1024 devices in a mesh: row: 16 (over y, x_lo), col: 64 (over z, x_hi, core).
Axes of the slice: x: 4 (x_hi: 2, x_lo: 2; x = x_hi * 2 + x_lo), y: 8, z: 16, core: 2. Of those that a mesh axis runs over, the one named last changes fastest.
Arguments:
- normed: bfloat16 [1024, 6144], P('col', 'row'), may hold values from -6 to 6
- upstream: bfloat16 [1024, 6144], P('col', 'row'), may hold values from -6 to 6
- loss_weight: float32 [1024], P('col'), may hold values from 0.05 to 0.5
- w_in: bfloat16 [6144, 24576], P('row', 'col'), may hold values from -0.078125 to 0.078125
- b_in: float32 [24576], P('col'), may hold values from -3 to 3
- w_out: bfloat16 [24576, 6144], P('col', 'row'), may hold values from -0.0390625 to 0.0390625
Outputs:
- grad_normed: bfloat16 [1024, 6144], P('col', 'row')
- grad_w_in: float32 [6144, 24576], P('row', 'col')
- grad_b_in: float32 [24576], P('col')
- grad_w_out: float32 [24576, 6144], P('col', 'row')
The draws below stay inside these ranges and needn't reach their ends.
All inputs are finite; a program needn't handle non-finite values.
Results may differ from the reference program's by a relative error of at most 0.028.
Values may be sent and summed in bfloat16 or wider, within the bound.
A program may use at most 32 MiB of HBM per device.

```python
import math
import jax
import jax.numpy as jnp
from jax import lax

D = 6144
FF = 24576
TOKENS = 1024
N_ROW = 16


def steps_of(key, extent, split, low, high):
    def one(position, blocks):
        heights = jax.random.uniform(jax.random.fold_in(jax.random.fold_in(key, 6), position), (blocks,), jnp.float32, low / len(split), high / len(split))
        return jnp.repeat(jnp.exp(heights), extent[position] // blocks).reshape((-1,) + (1,) * (len(extent) - position - 1))

    loudness = one(*split[0])
    for cut in split[1:]:
        loudness = loudness * one(*cut)
    return loudness


def centred(own_key, extent, spread, most, cuts=(), kind=jnp.bfloat16):
    factor_of = steps_of(own_key, extent, cuts, -0.22, 0.18) if cuts else 1.0
    drawn = jax.random.normal(own_key, extent, jnp.float32) * spread * factor_of
    return jnp.minimum(jnp.maximum(drawn, -most), most).astype(kind)


def setup_inputs(seed: int = 0) -> dict:
    seeds = jax.random.split(jax.random.key(seed), 7)
    normed = centred(seeds[0], (TOKENS, D), 1.0, 6.0, ((0, 64), (1, 16)))
    upstream = centred(seeds[1], (TOKENS, D), 1.0, 6.0, ((0, 64), (1, 16)))
    loss_weight = jnp.clip(jnp.exp(math.log(0.5) - 2.3025851 * jax.random.uniform(seeds[2], (TOKENS,), jnp.float32) ** steps_of(seeds[2], (TOKENS,), ((0, 64),), -0.2, 0.2)), 0.05, 0.5)
    w_in = centred(seeds[3], (D, FF), D ** -0.5, 0.078125, ((0, 16), (1, 64)))
    b_in = centred(seeds[4], (FF,), 0.5, 3.0, ((0, 64),), jnp.float32)
    w_out = centred(seeds[5], (FF, D), FF ** -0.5, 0.0390625, ((0, 64), (1, 16)))
    return {"normed": normed, "upstream": upstream, "loss_weight": loss_weight, "w_in": w_in, "b_in": b_in, "w_out": w_out}


def gelu_exact(values):
    return jax.nn.gelu(values, approximate=False)

def reference(normed, upstream, loss_weight, w_in, b_in, w_out):
    weighted = (upstream.astype(jnp.float32) * loss_weight[:, None]).astype(jnp.bfloat16)
    slab_width = D // N_ROW
    h_slabs = normed.reshape(TOKENS, N_ROW, slab_width).transpose(1, 0, 2)
    g_slabs = weighted.reshape(TOKENS, N_ROW, slab_width).transpose(1, 0, 2)
    in_slabs = w_in.reshape(N_ROW, slab_width, FF)
    out_slabs = w_out.reshape(FF, N_ROW, slab_width).transpose(1, 0, 2)

    def accumulate(carry, pieces):
        h_piece, g_piece, in_piece, out_piece = pieces
        part_pre = jnp.dot(h_piece, in_piece, preferred_element_type=jnp.float32).astype(jnp.bfloat16)
        part_grad = lax.dot_general(g_piece, out_piece, (((1,), (1,)), ((), ())), preferred_element_type=jnp.float32).astype(jnp.bfloat16)
        part_pre, part_grad = lax.optimization_barrier((part_pre, part_grad))
        return ((carry[0] + part_pre.astype(jnp.float32), carry[1] + part_grad.astype(jnp.float32)), None)
    zeros = jnp.zeros((TOKENS, FF), jnp.float32)
    (pre_sum, grad_act), _ = lax.scan(accumulate, (zeros, zeros), (h_slabs, g_slabs, in_slabs, out_slabs))
    pre_act = pre_sum + b_in[None, :]
    activated, pullback = jax.vjp(gelu_exact, pre_act)
    grad_pre = pullback(grad_act)[0].astype(jnp.bfloat16)
    activated = activated.astype(jnp.bfloat16)
    grad_w_out = lax.dot_general(activated, weighted, (((0,), (0,)), ((), ())), preferred_element_type=jnp.float32)
    grad_w_in = lax.dot_general(normed, grad_pre, (((0,), (0,)), ((), ())), preferred_element_type=jnp.float32)
    grad_b_in = lax.optimization_barrier(jnp.sum(grad_pre.astype(jnp.float32), axis=0))
    grad_normed = lax.dot_general(grad_pre, w_in, (((1,), (1,)), ((), ())), preferred_element_type=jnp.float32).astype(jnp.bfloat16)
    return (grad_normed, grad_w_in, grad_b_in, grad_w_out)
```

```python
import functools
import math

import jax
import jax.numpy as jnp
from jax import lax
from jax.experimental import pallas as pl
from jax.experimental.pallas import tpu as pltpu
from jax.sharding import PartitionSpec as P

BF16 = jnp.bfloat16
F32 = jnp.float32


def copy_keys(ny, nz):
    chunks, half = nz // ny, ny // 2
    keys = [("az", s) for s in range(nz) if s != nz // 2]
    keys += [(kind, s) for kind in ("ax", "as") for s in range(nz)]
    for kind in ("c", "e"):
        for k in range(chunks):
            for way in (0, 1):
                for d in range(half, 0, -1):
                    keys += [(kind, k, way, d, j) for j in (0, 1) if d < half or j == way]
            keys.append((kind + "x", k))
    keys += [("gs", k, i) for k in range(chunks) for i in (0, 1)]
    keys += [("gz", s) for s in range(nz) if s != nz // 2]
    keys.append(("gx",))
    return {key: i for i, key in enumerate(keys)}


def kernel(ny, nz, blk, f, normed, upstream, loss_weight, w_in, b_in, w_out,
           o_normed, o_w_in, o_b_in, o_w_out,
           hg, part, ae, c_in, c_out, cx_out, cx_in, gn_keep, gn_give, gn_got, gs, gr, gx_out, gx_in,
           send_sem, recv_sem):
    ids = copy_keys(ny, nz)
    chunks, half, mid = nz // ny, ny // 2, nz // 2
    row, col = lax.axis_index("row"), lax.axis_index("col")
    y, xl = row // 2, row % 2
    z, low = col // 4, col % 4
    xh, core = low // 2, low % 2

    def at_z(o):
        return (row, lax.rem(z + (o + nz), nz) * 4 + low)

    def at_y(d):
        return (lax.rem(y + (d + ny), ny) * 2 + xl, col)

    x_lo_peer = (y * 2 + (1 - xl), col)
    x_hi_peer = (row, z * 4 + (1 - xh) * 2 + core)
    sibling = (row, z * 4 + xh * 2 + (1 - core))

    started = []

    def send(key, src, dst, device):
        copy = pltpu.make_async_remote_copy(
            src_ref=src, dst_ref=dst, send_sem=send_sem.at[ids[key]], recv_sem=recv_sem.at[ids[key]],
            device_id=device, device_id_type=pl.DeviceIdType.MESH)
        copy.start()
        started.append(copy)

    def arrived(key, dst):
        pltpu.make_async_remote_copy(
            src_ref=dst, dst_ref=dst, send_sem=send_sem.at[ids[key]], recv_sem=recv_sem.at[ids[key]],
            device_id=sibling, device_id_type=pl.DeviceIdType.MESH).wait_recv()

    barrier = pltpu.get_barrier_semaphore()
    peers = [at_y(1), at_y(-1), x_lo_peer, x_hi_peer, sibling]
    for d in range(1, mid + 1):
        peers += [at_z(d), at_z(-d)] if d < mid else [at_z(d)]
    for peer in peers:
        pl.semaphore_signal(barrier, inc=1, device_id=peer, device_id_type=pl.DeviceIdType.MESH)

    def tok(slot, rc=0, rx=0, n=1):
        return pl.ds((slot * 4 + rc * 2 + rx) * blk, n * blk)

    diagonal = lax.broadcasted_iota(jnp.int32, (blk, blk), 0) == lax.broadcasted_iota(jnp.int32, (blk, blk), 1)
    weight = jnp.sum(jnp.where(diagonal, jnp.broadcast_to(loss_weight[...], (blk, blk)), 0.0), axis=1, keepdims=True)
    hg[tok(mid), :f] = normed[...]
    hg[tok(mid), f:] = (upstream[...].astype(F32) * weight).astype(BF16)

    pl.semaphore_wait(barrier, len(peers))

    order = [o for d in range(1, mid + 1) for o in ((d, -d) if d < mid else (-d,))]
    own = hg.at[tok(mid)]
    for o in order:
        slot = (mid - o) % nz
        send(("az", slot), own, hg.at[tok(slot)], at_z(o))

    def a_x(slot):
        if slot != mid:
            arrived(("az", slot), hg.at[tok(slot)])
        send(("ax", slot), hg.at[tok(slot)], hg.at[tok(slot, rx=1)], x_hi_peer)

    def a_s(slot):
        arrived(("ax", slot), hg.at[tok(slot, rx=1)])
        send(("as", slot), hg.at[tok(slot, n=2)], hg.at[tok(slot, rc=1, n=2)], sibling)

    def a_end(slot):
        arrived(("as", slot), hg.at[tok(slot, rc=1, n=2)])

    slots_by_distance = [mid] + [(mid + o) % nz for o in order]
    base = [(mid - half + k * ny) % nz for k in range(chunks)]

    def slots_of(k):
        return [s for s in slots_by_distance if (s - base[k]) % nz < ny]

    def ranges(k):
        first = base[k]
        if first + ny <= nz:
            return [(first, ny)]
        return [(first, nz - first), (0, ny - (nz - first))]

    def products(k):
        for first, count in ranges(k):
            for s in range(first, first + count, max(1, half)):
                rows = pl.ds(s * 4 * blk, max(1, half) * 4 * blk)
                part[rows, :f] = jnp.dot(hg[rows, :f], w_in[...], preferred_element_type=F32).astype(BF16)
                part[rows, f:] = lax.dot_general(
                    hg[rows, f:], w_out[...], (((1,), (1,)), ((), ())), preferred_element_type=F32).astype(BF16)

    def owned(k, d, j):
        slot = lax.rem(base[k] + lax.rem(y + (d + ny), ny), nz)
        which = xl if j == 0 else 1 - xl
        return pl.ds(pl.multiple_of((slot * 2 + which) * (2 * blk), 2 * blk), 2 * blk)

    def stage(k, way, d, j):
        return pl.ds((((k * 2 + way) * half + d - 1) * 2 + j) * 2 * blk, 2 * blk)

    def c_step(k, d):
        for way, sign in ((0, 1), (1, -1)):
            for j in (0, 1) if d < half else (way,):
                if d == half or (d == half - 1 and j != way):
                    src = part.at[owned(k, sign * d, j)]
                else:
                    here = stage(k, way, d + 1, j)
                    arrived(("c", k, way, d + 1, j), c_in.at[here])
                    out = stage(k, way, d, j)
                    c_out[out, :] = (c_in[here, :].astype(F32) + part[owned(k, sign * d, j), :].astype(F32)).astype(BF16)
                    src = c_out.at[out]
                send(("c", k, way, d, j), src, c_in.at[stage(k, way, d, j)], at_y(sign))

    def c_total(k, j):
        total = part[owned(k, 0, j), :].astype(F32)
        for way in (0, 1):
            if half > 1 or j == way:
                here = stage(k, way, 1, j)
                arrived(("c", k, way, 1, j), c_in.at[here])
                total = total + c_in[here, :].astype(F32)
        return total

    def x_rows(k):
        return pl.ds(k * 2 * blk, 2 * blk)

    def c_cross(k):
        cx_out[x_rows(k), :] = c_total(k, 1).astype(BF16)
        send(("cx", k), cx_out.at[x_rows(k)], cx_in.at[x_rows(k)], x_lo_peer)

    def act(k):
        total = c_total(k, 0)
        arrived(("cx", k), cx_in.at[x_rows(k)])
        total = total + cx_in[x_rows(k), :].astype(F32)
        pre = total[:, :f] + b_in[...]
        cdf = 0.5 * (1.0 + lax.erf(pre * (1.0 / math.sqrt(2.0))))
        pdf = jnp.exp(-0.5 * pre * pre) * (1.0 / math.sqrt(2.0 * math.pi))
        mine = owned(k, 0, 0)
        ae[mine, :f] = (pre * cdf).astype(BF16)
        ae[mine, f:] = (total[:, f:] * (cdf + pre * pdf)).astype(BF16)
        e_send(k, 1, 0)
        send(("ex", k), ae.at[mine], ae.at[mine], x_lo_peer)

    def e_send(k, d, j):
        for way, sign in ((0, 1), (1, -1)):
            if d < half or j == way:
                rows = owned(k, -sign * (d - 1), j)
                if d > 1:
                    arrived(("e", k, way, d - 1, j), ae.at[rows])
                send(("e", k, way, d, j), ae.at[rows], ae.at[rows], at_y(sign))

    def e_cross(k):
        rows = owned(k, 0, 1)
        arrived(("ex", k), ae.at[rows])
        e_send(k, 1, 1)

    def e_step(k, d):
        e_send(k, d, 0)
        e_send(k, d, 1)

    def e_end(k):
        for way, sign in ((0, 1), (1, -1)):
            arrived(("e", k, way, half, way), ae.at[owned(k, -sign * half, way)])
            if half > 1:
                arrived(("e", k, way, half - 1, 1 - way), ae.at[owned(k, -sign * (half - 1), 1 - way)])

    def input_grad(k):
        for i, (first, count) in enumerate(ranges(k)):
            for s in range(first, first + count, max(1, half)):
                n = max(1, half)
                rows, kept = pl.ds(s * 4 * blk, n * 4 * blk), pl.ds(s * 2 * blk, n * 2 * blk)
                got = lax.dot_general(ae[rows, f:], w_in[...], (((1,), (1,)), ((), ())), preferred_element_type=F32)
                got = got.reshape(n, 2, 2 * blk, f)
                gn_keep[kept, :] = got[:, 0].reshape(n * 2 * blk, f)
                gn_give[kept, :] = got[:, 1].reshape(n * 2 * blk, f).astype(BF16)
            span = pl.ds(first * 2 * blk, count * 2 * blk)
            send(("gs", k, i), gn_give.at[span], gn_got.at[span], sibling)

    def g_send(k):
        for i, (first, count) in enumerate(ranges(k)):
            span = pl.ds(first * 2 * blk, count * 2 * blk)
            arrived(("gs", k, i), gn_got.at[span])
            gn_keep[span, :] = gn_keep[span, :] + gn_got[span, :].astype(F32)
            gs[span, :] = gn_keep[span, :].astype(BF16)
        for slot in reversed(slots_of(k)):
            if slot != mid:
                there = (2 * mid - slot) % nz
                send(("gz", there), gs.at[pl.ds(slot * 2 * blk, 2 * blk)], gr.at[pl.ds(there * 2 * blk, 2 * blk)],
                     at_z(slot - mid))

    def weight_grads(k):
        for i, (first, count) in enumerate(ranges(k)):
            rows = pl.ds(first * 4 * blk, count * 4 * blk)
            h, g = hg[rows, :f], hg[rows, f:]
            a, e = ae[rows, :f], ae[rows, f:]
            w_o = lax.dot_general(a, g, (((0,), (0,)), ((), ())), preferred_element_type=F32)
            w_i = lax.dot_general(h, e, (((0,), (0,)), ((), ())), preferred_element_type=F32)
            b = jnp.sum(e.astype(F32), axis=0, keepdims=True)
            if k == 0 and i == 0:
                o_w_out[...], o_w_in[...], o_b_in[...] = w_o, w_i, b
            else:
                o_w_out[...] += w_o
                o_w_in[...] += w_i
                o_b_in[...] += b

    def g_end():
        total = gn_keep[pl.ds(mid * 2 * blk, 2 * blk), :]
        for s in slots_by_distance[1:]:
            rows = pl.ds(s * 2 * blk, 2 * blk)
            arrived(("gz", s), gr.at[rows])
            total = total + gr[rows, :].astype(F32)
        gx_out[...] = total[blk:].astype(BF16)
        send(("gx",), gx_out, gx_in, x_hi_peer)
        arrived(("gx",), gx_in)
        o_normed[...] = (total[:blk] + gx_in[...].astype(F32)).astype(BF16)

    def gather_chunk(k):
        for s in slots_of(k):
            a_x(s)

    def spread_chunk(k):
        for s in slots_of(k):
            a_s(s)

    gather_chunk(0)
    spread_chunk(0)
    for s in slots_of(0):
        a_end(s)
    for k in range(chunks):
        products(k)
        c_step(k, half)
        if half > 1:
            c_step(k, half - 1)
        if k + 1 < chunks:
            gather_chunk(k + 1)
            spread_chunk(k + 1)
            for s in slots_of(k + 1):
                a_end(s)
    for d in range(half - 2, 0, -1):
        for k in range(chunks):
            c_step(k, d)
    for k in range(chunks):
        c_cross(k)
    for k in range(chunks):
        act(k)
    for k in range(chunks):
        e_cross(k)
    for d in range(2, half + 1):
        for k in range(chunks):
            e_step(k, d)
    for k in range(chunks):
        e_end(k)
        input_grad(k)
    for k in range(chunks):
        g_send(k)
    for k in range(chunks):
        weight_grads(k)
    g_end()
    for copy in started:
        copy.wait_send()


def on_device(ny, nz, normed, upstream, loss_weight, w_in, b_in, w_out):
    blk, f = normed.shape
    chunks, half = nz // ny, ny // 2
    n = len(copy_keys(ny, nz))
    all_rows = 4 * nz * blk
    stages = chunks * 2 * half * 2 * 2 * blk
    vmem = pl.BlockSpec(memory_space=pltpu.VMEM)
    outs = pl.pallas_call(
        functools.partial(kernel, ny, nz, blk, f),
        out_shape=(
            jax.ShapeDtypeStruct((blk, f), BF16),
            jax.ShapeDtypeStruct(w_in.shape, F32),
            jax.ShapeDtypeStruct((1, w_in.shape[1]), F32),
            jax.ShapeDtypeStruct(w_out.shape, F32),
        ),
        in_specs=[vmem] * 6,
        out_specs=(vmem,) * 4,
        scratch_shapes=[
            pltpu.VMEM((all_rows, 2 * f), BF16),
            pltpu.VMEM((all_rows, 2 * f), BF16),
            pltpu.VMEM((all_rows, 2 * f), BF16),
            pltpu.VMEM((stages, 2 * f), BF16),
            pltpu.VMEM((stages, 2 * f), BF16),
            pltpu.VMEM((chunks * 2 * blk, 2 * f), BF16),
            pltpu.VMEM((chunks * 2 * blk, 2 * f), BF16),
            pltpu.VMEM((all_rows // 2, f), F32),
            pltpu.VMEM((all_rows // 2, f), BF16),
            pltpu.VMEM((all_rows // 2, f), BF16),
            pltpu.VMEM((all_rows // 2, f), BF16),
            pltpu.VMEM((all_rows // 2, f), BF16),
            pltpu.VMEM((blk, f), BF16),
            pltpu.VMEM((blk, f), BF16),
            pltpu.SemaphoreType.DMA((n,)),
            pltpu.SemaphoreType.DMA((n,)),
        ],
        compiler_params=pltpu.CompilerParams(
            collective_id=0, has_side_effects=True, vmem_limit_bytes=48 * 2**20),
        name="mlp_backward",
    )(normed, upstream, loss_weight.reshape(1, blk), w_in, b_in.reshape(1, -1), w_out)
    return outs[0], outs[1], outs[2].reshape(-1), outs[3]


def solution(mesh):
    ny, nz = mesh.shape["row"] // 2, mesh.shape["col"] // 4
    return jax.shard_map(
        functools.partial(on_device, ny, nz),
        mesh=mesh,
        in_specs=(P("col", "row"), P("col", "row"), P("col"), P("row", "col"), P("col"), P("col", "row")),
        out_specs=(P("col", "row"), P("row", "col"), P("col"), P("col", "row")),
        check_vma=False,
    )
```

```python
import functools
import math

import jax
import jax.numpy as jnp
from jax import lax
from jax.experimental import pallas as pl
from jax.experimental.pallas import tpu as pltpu
from jax.sharding import PartitionSpec as P

BF16 = jnp.bfloat16
F32 = jnp.float32
MESH = pl.DeviceIdType.MESH


def copy_keys(ny, nz):
    half, reach = ny // 2, nz // 4
    ways = (0, 1)
    keys = [("wi",), ("wo",), ("al",)]
    keys += [("az", s, rx) for rx in ways for s in range(1, nz) if s != nz // 2]
    keys += [("az", 0, rx, way) for rx in ways for way in ways]
    keys += [("al", nz // 2 + s * d) for d in range(1, reach + 1) for s in (1, -1)]
    keys += [("ax", nz // 2 + d) for d in range(-reach, reach + 1)] + [("as", s) for s in range(nz)]
    keys += [(kind, way, i) for kind in ("c1", "c2", "e1", "e2") for way in ways for i in range(1, half // 2 + 1)]
    keys += [("gs", i) for i in ways]
    keys += [(kind, way, i) for kind in ("g1", "g2") for way in ways for i in range(1, reach + 1)]
    keys += [("gx",), ("gl",), ("gd",), ("vi",), ("vo",), ("vb",)]
    return {key: i for i, key in enumerate(keys)}


def kernel(ny, nz, blk, f, normed_hbm, upstream_hbm, loss_weight_hbm, w_in_hbm, b_in_hbm, w_out_hbm,
           o_normed, o_w_in, o_b_in, o_w_out,
           normed, upstream, loss_weight, b_in, w_in, w_out, w_in2, w_out2,
           hg, al_out, part, ae, c1_in, c2_out, c2_in, gn, gn_give, gn_got, gs, g1_in, g2_out, g2_in, g_out, gx_in, gl_in, gd_in,
           vi_out, vi_in, vo_out, vo_in, vb_out, vb_in, load_sem, send_sem, recv_sem):
    ids = copy_keys(ny, nz)
    half, mid, reach = ny // 2, nz // 2, nz // 4
    hop = half // 2
    row, col = lax.axis_index("row"), lax.axis_index("col")
    y, xl = row // 2, row % 2
    z, low = col // 4, col % 4
    xh, core = low // 2, low % 2
    busy = core == xl
    idle = core != xl
    signs = ((0, 1), (1, -1))

    def at_z(o):
        return (row, lax.rem(z + (o + nz), nz) * 4 + low)

    def at_y(d):
        return (lax.rem(y + (d + ny), ny) * 2 + xl, col)

    x_lo_peer = (y * 2 + (1 - xl), col)
    x_hi_peer = (row, z * 4 + (1 - xh) * 2 + core)
    x_both_peer = (y * 2 + (1 - xl), z * 4 + (1 - xh) * 2 + core)
    sibling = (row, z * 4 + xh * 2 + (1 - core))

    sent = {"all": [], "busy": [], "idle": []}

    def send(key, src, dst, device, who="all"):
        pltpu.make_async_remote_copy(
            src_ref=src, dst_ref=dst, send_sem=send_sem.at[ids[key]], recv_sem=recv_sem.at[ids[key]],
            device_id=device, device_id_type=MESH).start()
        sent[who].append((key, src))

    def handle(key, ref):
        return pltpu.make_async_remote_copy(
            src_ref=ref, dst_ref=ref, send_sem=send_sem.at[ids[key]], recv_sem=recv_sem.at[ids[key]],
            device_id=sibling, device_id_type=MESH)

    def arrived(key, dst):
        handle(key, dst).wait_recv()

    barrier = pltpu.get_barrier_semaphore()
    toward = [s * d for d in range(reach, 0, -1) for s in (1, -1)]
    near = [at_y(sign * d) for d in range(1, hop + 1) for sign in (1, -1)]
    near += [x_lo_peer, x_hi_peer, x_both_peer, sibling]
    along_z = [at_z(o) for o in toward]
    slanted = [(y * 2 + (1 - xl), at_z(o)[1]) for o in toward]
    for peer in slanted + near:
        pl.semaphore_signal(barrier, inc=1, device_id=peer, device_id_type=MESH)

    @pl.when(busy)
    def _():
        for peer in along_z:
            pl.semaphore_signal(barrier, inc=1, device_id=peer, device_id_type=MESH)

    pairs = ((normed_hbm, normed), (upstream_hbm, upstream), (loss_weight_hbm, loss_weight), (b_in_hbm, b_in),
             (w_in_hbm, w_in), (w_out_hbm, w_out))
    loads = [pltpu.make_async_copy(src, dst, load_sem.at[i]) for i, (src, dst) in enumerate(pairs)]
    for load in loads:
        load.start()
    for load in loads[:4]:
        load.wait()

    def tok(slot, rx=0, n=1):
        return pl.ds((slot * 2 + rx) * blk, n * blk)

    diagonal = lax.broadcasted_iota(jnp.int32, (blk, blk), 0) == lax.broadcasted_iota(jnp.int32, (blk, blk), 1)
    weight = jnp.sum(jnp.where(diagonal, jnp.broadcast_to(loss_weight[...], (blk, blk)), 0.0), axis=1, keepdims=True)
    weighted = (upstream[...].astype(F32) * weight).astype(BF16)

    slab0, slab1 = pl.ds(0, 2 * f), pl.ds(2 * f, 2 * f)
    first_slots = [mid + s * d for d in range(1, reach) for s in (1, -1)]
    far_slots = [mid + s * d for d in range(reach + 1, mid) for s in (1, -1)] + [0]
    edge_slots = [mid - reach, mid + reach]

    @pl.when(idle)
    def _():
        al_out[:, :f] = normed[...]
        al_out[:, f:] = weighted
        pl.semaphore_wait(barrier, len(near) + len(slanted))
        for o, peer in zip(toward, slanted):
            send(("al", mid - o), al_out, hg.at[tok(mid - o), slab1], peer, "idle")
        send(("al",), al_out, hg.at[tok(mid), slab1], x_lo_peer, "idle")
        send(("wi",), w_in_hbm, w_in2, x_lo_peer, "idle")
        send(("wo",), w_out_hbm, w_out2, x_lo_peer, "idle")

    @pl.when(busy)
    def _():
        hg[tok(mid), slab0] = jnp.concatenate([normed[...], weighted], axis=1)
        pl.semaphore_wait(barrier, len(near) + len(slanted) + len(along_z))
        for o, peer in zip(toward, along_z):
            send(("az", mid - o, 0), hg.at[tok(mid), slab0], hg.at[tok(mid - o), slab0], peer, "busy")

    def relay(way, sign, rx):
        slot = mid - sign * reach
        for d in range(reach, 0, -1):
            there = (slot - sign * d) % nz
            src, dst = tok(slot, rx), tok(there, rx)
            if d < reach:
                send(("az", there, rx), hg.at[src], hg.at[dst], at_z(sign * d), "busy")
            else:
                lanes = pl.ds(2 * f * way, 2 * f)
                send(("az", 0, rx, way), hg.at[src, lanes], hg.at[dst, lanes], at_z(sign * d), "busy")

    @pl.when(busy)
    def _():
        def meet(slot):
            if slot != mid:
                arrived(("az", slot, 0), hg.at[tok(slot), slab0])
            arrived(("al",) if slot == mid else ("al", slot), hg.at[tok(slot), slab1])
            send(("ax", slot), hg.at[tok(slot)], hg.at[tok(slot, rx=1)], x_hi_peer, "busy")

        def down(slot):
            send(("as", slot), hg.at[tok(slot, n=2)], hg.at[tok(slot, n=2)], sibling, "busy")

        for way, sign in signs:
            meet(mid - sign * reach)
            relay(way, sign, 0)
        for s in [mid] + first_slots:
            meet(s)
        send(("wi",), w_in_hbm, w_in2, x_lo_peer, "busy")
        send(("wo",), w_out_hbm, w_out2, x_lo_peer, "busy")
        for way, sign in signs:
            slot = mid - sign * reach
            arrived(("ax", slot), hg.at[tok(slot, rx=1)])
            relay(way, sign, 1)
            down(slot)
        for s in [mid] + first_slots:
            arrived(("ax", s), hg.at[tok(s, rx=1)])
            down(s)
        for s in far_slots:
            for rx in (0, 1):
                if s == 0:
                    for way in (0, 1):
                        arrived(("az", 0, rx, way), hg.at[tok(0, rx), pl.ds(2 * f * way, 2 * f)])
                else:
                    arrived(("az", s, rx), hg.at[tok(s, rx)])
            down(s)

    @pl.when(idle)
    def _():
        for s in range(nz):
            arrived(("as", s), hg.at[tok(s, n=2)])

    def products():
        part[:, :f] = (jnp.dot(hg[:, :f], w_in[...], preferred_element_type=F32)
                       + jnp.dot(hg[:, 2 * f:3 * f], w_in2[...], preferred_element_type=F32)).astype(BF16)
        turned = (((1,), (1,)), ((), ()))
        part[:, f:] = (
            lax.dot_general(hg[:, f:2 * f], w_out[...], turned, preferred_element_type=F32)
            + lax.dot_general(hg[:, 3 * f:], w_out2[...], turned, preferred_element_type=F32)).astype(BF16)

    share = 2 * nz * blk // ny

    def owned(d, j=None):
        start = lax.rem(y + (d + ny), ny) * share
        if j is None:
            return pl.ds(pl.multiple_of(start, share), share)
        return pl.ds(pl.multiple_of(start + j * (share // 2), share // 2), share // 2)

    def stage(way, i, j=None):
        start = (way * hop + i - 1) * share
        return pl.ds(start, share) if j is None else pl.ds(start + j * (share // 2), share // 2)

    def c_first():
        for i in range(hop, 0, -1):
            for way, sign in signs:
                j = way if i == hop else None
                send(("c1", way, i), part.at[owned(sign * (hop + i), j)], c1_in.at[stage(way, i, j)], at_y(sign * i))
        for i in range(hop - 1, 0, -1):
            for way, sign in signs:
                send(("c2", way, i), part.at[owned(sign * i)], c2_in.at[stage(way, i)], at_y(sign * i))

    def c_relay():
        for way, sign in signs:
            out = pl.ds(way * share, share)
            last = stage(way, hop, way)
            total = part[owned(sign * hop), :].astype(F32)
            for i in range(1, hop):
                arrived(("c1", way, i), c1_in.at[stage(way, i)])
                total = total + c1_in[stage(way, i), :].astype(F32)
            arrived(("c1", way, hop), c1_in.at[last])
            c2_out[out, :] = total.astype(BF16)
            lo = way * (share // 2)
            c2_out[pl.ds(way * share + lo, share // 2), :] = (
                total[lo:lo + share // 2] + c1_in[last, :].astype(F32)).astype(BF16)
            send(("c2", way, hop), c2_out.at[out], c2_in.at[stage(way, hop)], at_y(sign * hop))

    def act():
        mine = owned(0)
        total = part[mine, :].astype(F32)
        for i in range(1, hop + 1):
            for way in (0, 1):
                arrived(("c2", way, i), c2_in.at[stage(way, i)])
                total = total + c2_in[stage(way, i), :].astype(F32)
        pre = total[:, :f] + b_in[...].reshape(1, f)
        cdf = 0.5 * (1.0 + lax.erf(pre * (1.0 / math.sqrt(2.0))))
        pdf = jnp.exp(-0.5 * pre * pre) * (1.0 / math.sqrt(2.0 * math.pi))
        ae[mine, :f] = (pre * cdf).astype(BF16)
        ae[mine, f:] = (total[:, f:] * (cdf + pre * pdf)).astype(BF16)
        for i in range(hop, 0, -1):
            for way, sign in signs:
                send(("e1", way, i), ae.at[mine], ae.at[mine], at_y(sign * i))

    def e_relay():
        for way, sign in signs:
            arrived(("e1", way, hop), ae.at[owned(-sign * hop)])
            for d in range(hop, 0, -1):
                rows = owned(-sign * hop, way if d == hop else None)
                send(("e2", way, d), ae.at[rows], ae.at[rows], at_y(sign * d))

    def e_end():
        for way, sign in signs:
            for i in range(1, hop):
                arrived(("e1", way, i), ae.at[owned(-sign * i)])
            for d in range(1, hop + 1):
                arrived(("e2", way, d), ae.at[owned(-sign * (hop + d), way if d == hop else None)])

    pieces = [(i, pl.ds(i * nz * blk, nz * blk)) for i in (0, 1)]

    def input_grad():
        turned = (((1,), (1,)), ((), ()))
        for i, rows in pieces:
            own = lax.dot_general(ae[rows, f:], w_in[...], turned, preferred_element_type=F32)
            other = lax.dot_general(ae[rows, f:], w_in2[...], turned, preferred_element_type=F32)

            @pl.when(busy)
            def _():
                gn[rows, :f] = own
                gn[rows, f:] = other

            @pl.when(idle)
            def _():
                gn_give[rows, :f] = own.astype(BF16)
                gn_give[rows, f:] = other.astype(BF16)
                send(("gs", i), gn_give.at[rows], gn_got.at[rows], sibling, "idle")

    def g_first():
        for i, rows in pieces:
            arrived(("gs", i), gn_got.at[rows])
            gn[rows, :] = gn[rows, :] + gn_got[rows, :].astype(F32)
            gs[rows, :] = gn[rows, :].astype(BF16)

    def g_rows(way, i, j=None):
        start = (way * reach + i - 1) * 2 * blk
        return pl.ds(start, 2 * blk) if j is None else pl.ds(start + j * blk, blk)

    def g_send():
        for i in range(reach, 0, -1):
            for way, sign in signs:
                slot = (mid + sign * (reach + i)) % nz
                src, dst = (tok(slot, n=2), g_rows(way, i)) if i < reach else (tok(slot, rx=way), g_rows(way, i, way))
                send(("g1", way, i), gs.at[src], g1_in.at[dst], at_z(sign * i), "busy")
        for i in range(reach - 1, 0, -1):
            for way, sign in signs:
                send(("g2", way, i), gs.at[tok(mid + sign * i, n=2)], g2_in.at[g_rows(way, i)], at_z(sign * i), "busy")

    def g_relay():
        for way, sign in signs:
            total = gn[tok(mid + sign * reach, n=2), :]
            for i in range(1, reach):
                arrived(("g1", way, i), g1_in.at[g_rows(way, i)])
                total = total + g1_in[g_rows(way, i), :].astype(F32)
            last = g_rows(way, reach, way)
            arrived(("g1", way, reach), g1_in.at[last])
            there, out = g_rows(way, reach), pl.ds(way * 2 * blk, 2 * blk)
            g2_out[out, :] = total.astype(BF16)
            half_rows = pl.ds((way * 2 + way) * blk, blk)
            g2_out[half_rows, :] = (total[way * blk:(way + 1) * blk] + g1_in[last, :].astype(F32)).astype(BF16)
            send(("g2", way, reach), g2_out.at[out], g2_in.at[there], at_z(sign * reach), "busy")

    def g_end():
        total = gn[tok(mid, n=2), :]
        for i in range(1, reach + 1):
            for way in (0, 1):
                arrived(("g2", way, i), g2_in.at[g_rows(way, i)])
                total = total + g2_in[g_rows(way, i), :].astype(F32)
        g_out[...] = total.astype(BF16)
        send(("gx",), g_out.at[pl.ds(blk, blk), pl.ds(0, f)], gx_in, x_hi_peer, "busy")
        send(("gl",), g_out.at[pl.ds(0, blk), pl.ds(f, f)], gl_in, x_lo_peer, "busy")
        send(("gd",), g_out.at[pl.ds(blk, blk), pl.ds(f, f)], gd_in, x_both_peer, "busy")
        arrived(("gx",), gx_in)
        o_normed[...] = (total[:blk, :f] + gx_in[...].astype(F32)).astype(BF16)

    down_rows = (((0,), (0,)), ((), ()))

    def other_weight_grads():
        a, e = ae[:, :f], ae[:, f:]
        vo_out[...] = lax.dot_general(a, hg[:, 3 * f:], down_rows, preferred_element_type=F32).astype(BF16)
        send(("vo",), vo_out, vo_in, x_lo_peer)
        vi_out[...] = lax.dot_general(hg[:, 2 * f:3 * f], e, down_rows, preferred_element_type=F32).astype(BF16)
        send(("vi",), vi_out, vi_in, x_lo_peer)
        vb_out[...] = jnp.broadcast_to(jnp.sum(e.astype(F32), axis=0, keepdims=True), (8, f))
        send(("vb",), vb_out, vb_in, x_lo_peer)

    def weight_grads():
        a, e = ae[:, :f], ae[:, f:]
        o_w_out[...] = lax.dot_general(a, hg[:, f:2 * f], down_rows, preferred_element_type=F32)
        o_w_in[...] = lax.dot_general(hg[:, :f], e, down_rows, preferred_element_type=F32)

    def weight_grads_end():
        arrived(("vo",), vo_in)
        o_w_out[...] += vo_in[...].astype(F32)
        arrived(("vi",), vi_in)
        o_w_in[...] += vi_in[...].astype(F32)
        arrived(("vb",), vb_in)
        o_b_in[...] = (vb_out[:1, :] + vb_in[:1, :]).reshape(f)

    for load in loads[4:]:
        load.wait()
    arrived(("wi",), w_in2)
    arrived(("wo",), w_out2)
    products()
    c_first()
    c_relay()
    act()
    e_relay()
    e_end()
    input_grad()

    @pl.when(busy)
    def _():
        g_first()
        g_send()

    other_weight_grads()

    @pl.when(busy)
    def _():
        g_relay()

    weight_grads()
    weight_grads_end()

    @pl.when(busy)
    def _():
        g_end()

    @pl.when(idle)
    def _():
        arrived(("gl",), gl_in)
        arrived(("gd",), gd_in)
        o_normed[...] = (gl_in[...].astype(F32) + gd_in[...].astype(F32)).astype(BF16)
        for key, src in sent["idle"]:
            handle(key, src).wait_send()

    @pl.when(busy)
    def _():
        for key, src in sent["busy"]:
            handle(key, src).wait_send()

    for key, src in sent["all"]:
        handle(key, src).wait_send()


def on_device(ny, nz, normed, upstream, loss_weight, w_in, b_in, w_out):
    blk, f = normed.shape
    half, reach = ny // 2, nz // 4
    n = len(copy_keys(ny, nz))
    rows = 2 * nz * blk
    share = rows // ny
    vmem, hbm = pl.BlockSpec(memory_space=pltpu.VMEM), pl.BlockSpec(memory_space=pl.ANY)
    outs = pl.pallas_call(
        functools.partial(kernel, ny, nz, blk, f),
        out_shape=(
            jax.ShapeDtypeStruct((blk, f), BF16),
            jax.ShapeDtypeStruct(w_in.shape, F32),
            jax.ShapeDtypeStruct((f,), F32),
            jax.ShapeDtypeStruct(w_out.shape, F32),
        ),
        in_specs=[hbm] * 6,
        out_specs=(vmem,) * 4,
        scratch_shapes=[
            pltpu.VMEM((blk, f), BF16),
            pltpu.VMEM((blk, f), BF16),
            pltpu.VMEM((1, blk), F32),
            pltpu.VMEM((f,), F32),
            pltpu.VMEM((f, f), BF16),
            pltpu.VMEM((f, f), BF16),
            pltpu.VMEM((f, f), BF16),
            pltpu.VMEM((f, f), BF16),
            pltpu.VMEM((rows, 4 * f), BF16),
            pltpu.VMEM((blk, 2 * f), BF16),
            pltpu.VMEM((rows, 2 * f), BF16),
            pltpu.VMEM((rows, 2 * f), BF16),
            pltpu.VMEM((half * share, 2 * f), BF16),
            pltpu.VMEM((2 * share, 2 * f), BF16),
            pltpu.VMEM((half * share, 2 * f), BF16),
            pltpu.VMEM((rows, 2 * f), F32),
            pltpu.VMEM((rows, 2 * f), BF16),
            pltpu.VMEM((rows, 2 * f), BF16),
            pltpu.VMEM((rows, 2 * f), BF16),
            pltpu.VMEM((2 * reach * 2 * blk, 2 * f), BF16),
            pltpu.VMEM((2 * 2 * blk, 2 * f), BF16),
            pltpu.VMEM((2 * reach * 2 * blk, 2 * f), BF16),
            pltpu.VMEM((2 * blk, 2 * f), BF16),
            pltpu.VMEM((blk, f), BF16),
            pltpu.VMEM((blk, f), BF16),
            pltpu.VMEM((blk, f), BF16),
            pltpu.VMEM((f, f), BF16),
            pltpu.VMEM((f, f), BF16),
            pltpu.VMEM((f, f), BF16),
            pltpu.VMEM((f, f), BF16),
            pltpu.VMEM((8, f), F32),
            pltpu.VMEM((8, f), F32),
            pltpu.SemaphoreType.DMA((6,)),
            pltpu.SemaphoreType.DMA((n,)),
            pltpu.SemaphoreType.DMA((n,)),
        ],
        compiler_params=pltpu.CompilerParams(
            collective_id=0, has_side_effects=True, vmem_limit_bytes=60 * 2**20),
        name="mlp_backward",
    )(normed, upstream, loss_weight.reshape(1, blk), w_in, b_in, w_out)
    return outs[0], outs[1], outs[2], outs[3]


def solution(mesh):
    ny, nz = mesh.shape["row"] // 2, mesh.shape["col"] // 4
    return jax.shard_map(
        functools.partial(on_device, ny, nz),
        mesh=mesh,
        in_specs=(P("col", "row"), P("col", "row"), P("col"), P("row", "col"), P("col"), P("col", "row")),
        out_specs=(P("col", "row"), P("row", "col"), P("col"), P("col", "row")),
        check_vma=False,
    )
```

```python
import functools
import math

import jax
import jax.numpy as jnp
from jax import lax
from jax.experimental import pallas as pl
from jax.experimental.pallas import tpu as pltpu
from jax.sharding import PartitionSpec as P

BF16 = jnp.bfloat16
F32 = jnp.float32
MESH = pl.DeviceIdType.MESH


def copy_keys(ny, nz):
    half, reach = ny // 2, nz // 4
    ways = (0, 1)
    keys = [("wi",), ("wo",), ("al",)]
    keys += [("az", s, rx) for rx in ways for s in range(1, nz) if s != nz // 2]
    keys += [("az", 0, rx, way) for rx in ways for way in ways]
    keys += [("al", nz // 2 + s * d) for d in range(1, reach + 1) for s in (1, -1)]
    keys += [("ax", nz // 2 + d) for d in range(-reach, reach + 1)] + [("as", i) for i in range(3)]
    keys += [(kind, way, i) for kind in ("c1", "c2", "e1", "e2") for way in ways for i in range(1, half // 2 + 1)]
    keys += [("gs", d % ny) for d in range(ny)]
    keys += [(kind, way, i) for kind in ("g1", "g2") for way in ways for i in range(1, reach + 1)]
    keys += [("gx",), ("gl",), ("vi",), ("vo",), ("vb",)]
    return {key: i for i, key in enumerate(keys)}


def kernel(ny, nz, blk, f, normed_hbm, upstream_hbm, loss_weight_hbm, w_in_hbm, b_in_hbm, w_out_hbm,
           o_normed, o_w_in, o_b_in, o_w_out,
           normed, upstream, loss_weight, b_in, w_in, w_out, w_in2, w_out2, turned_in,
           hg, al_out, part, ae, c1_in, c2_out, c2_in, gn, gn_give, gn_got, gs, g1_in, g2_out, g2_in, g_out, gx_in, gl_in,
           vi_out, vi_in, vo_out, vo_in, vb_out, vb_in, load_sem, send_sem, recv_sem):
    ids = copy_keys(ny, nz)
    half, mid, reach = ny // 2, nz // 2, nz // 4
    hop = half // 2
    row, col = lax.axis_index("row"), lax.axis_index("col")
    y, xl = row // 2, row % 2
    z, low = col // 4, col % 4
    xh, core = low // 2, low % 2
    busy = core == xl
    idle = core != xl
    signs = ((0, 1), (1, -1))

    def at_z(o):
        return (row, lax.rem(z + (o + nz), nz) * 4 + low)

    def at_y(d):
        return (lax.rem(y + (d + ny), ny) * 2 + xl, col)

    x_lo_peer = (y * 2 + (1 - xl), col)
    x_hi_peer = (row, z * 4 + (1 - xh) * 2 + core)
    cross_lo = (y * 2 + (1 - xl), z * 4 + xh * 2 + (1 - core))
    cross_both = (y * 2 + (1 - xl), z * 4 + (1 - xh) * 2 + (1 - core))
    sibling = (row, z * 4 + xh * 2 + (1 - core))

    sent = {"all": [], "busy": [], "idle": []}

    def send(key, src, dst, device, who="all"):
        pltpu.make_async_remote_copy(
            src_ref=src, dst_ref=dst, send_sem=send_sem.at[ids[key]], recv_sem=recv_sem.at[ids[key]],
            device_id=device, device_id_type=MESH).start()
        sent[who].append((key, src))

    def handle(key, ref):
        return pltpu.make_async_remote_copy(
            src_ref=ref, dst_ref=ref, send_sem=send_sem.at[ids[key]], recv_sem=recv_sem.at[ids[key]],
            device_id=sibling, device_id_type=MESH)

    def arrived(key, dst):
        handle(key, dst).wait_recv()

    barrier = pltpu.get_barrier_semaphore()
    toward = [s * d for d in range(reach, 0, -1) for s in (1, -1)]
    near = [at_y(sign * d) for d in range(1, hop + 1) for sign in (1, -1)]
    near += [x_lo_peer, x_hi_peer, sibling] + [at_z(o) for o in toward]
    along_z = [at_z(o) for o in toward]
    slanted = [(y * 2 + (1 - xl), at_z(o)[1]) for o in toward]
    crossed = [cross_lo, cross_both]
    for peer in slanted + near:
        pl.semaphore_signal(barrier, inc=1, device_id=peer, device_id_type=MESH)

    @pl.when(idle)
    def _():
        for peer in crossed:
            pl.semaphore_signal(barrier, inc=1, device_id=peer, device_id_type=MESH)

    pairs = ((normed_hbm, normed), (upstream_hbm, upstream), (loss_weight_hbm, loss_weight), (b_in_hbm, b_in),
             (w_in_hbm, w_in), (w_out_hbm, w_out))
    loads = [pltpu.make_async_copy(src, dst, load_sem.at[i]) for i, (src, dst) in enumerate(pairs)]
    for load in loads:
        load.start()
    for load in loads[:4]:
        load.wait()

    def tok(slot, rx=0, n=1):
        return pl.ds((slot * 2 + rx) * blk, n * blk)

    diagonal = lax.broadcasted_iota(jnp.int32, (blk, blk), 0) == lax.broadcasted_iota(jnp.int32, (blk, blk), 1)
    weight = jnp.sum(jnp.where(diagonal, jnp.broadcast_to(loss_weight[...], (blk, blk)), 0.0), axis=1, keepdims=True)
    weighted = (upstream[...].astype(F32) * weight).astype(BF16)

    slab0, slab1 = pl.ds(0, 2 * f), pl.ds(2 * f, 2 * f)
    first_slots = [mid + s * d for d in range(1, reach) for s in (1, -1)]
    spans = [(mid - reach, 2 * reach + 1), (mid + reach + 1, mid - reach - 1), (0, mid - reach)]

    @pl.when(idle)
    def _():
        al_out[:, :f] = normed[...]
        al_out[:, f:] = weighted
        pl.semaphore_wait(barrier, len(near) + len(slanted) + len(crossed))
        for o, peer in zip(toward, slanted):
            send(("al", mid - o), al_out, hg.at[tok(mid - o), slab1], peer, "idle")
        send(("al",), al_out, hg.at[tok(mid), slab1], x_lo_peer, "idle")
        send(("wi",), w_in_hbm, w_in2, x_lo_peer, "idle")
        send(("wo",), w_out_hbm, w_out2, x_lo_peer, "idle")

    @pl.when(busy)
    def _():
        hg[tok(mid), slab0] = jnp.concatenate([normed[...], weighted], axis=1)
        pl.semaphore_wait(barrier, len(near) + len(slanted))
        for o, peer in zip(toward, along_z):
            send(("az", mid - o, 0), hg.at[tok(mid), slab0], hg.at[tok(mid - o), slab0], peer, "busy")

    def relay(way, sign, rx):
        slot = mid - sign * reach
        for d in range(reach, 0, -1):
            there = (slot - sign * d) % nz
            src, dst = tok(slot, rx), tok(there, rx)
            if d < reach:
                send(("az", there, rx), hg.at[src], hg.at[dst], at_z(sign * d), "busy")
            else:
                lanes = pl.ds(2 * f * way, 2 * f)
                send(("az", 0, rx, way), hg.at[src, lanes], hg.at[dst, lanes], at_z(sign * d), "busy")

    @pl.when(busy)
    def _():
        def meet(slot):
            if slot != mid:
                arrived(("az", slot, 0), hg.at[tok(slot), slab0])
            arrived(("al",) if slot == mid else ("al", slot), hg.at[tok(slot), slab1])
            send(("ax", slot), hg.at[tok(slot)], hg.at[tok(slot, rx=1)], x_hi_peer, "busy")

        def down(i):
            rows = tok(spans[i][0], n=2 * spans[i][1])
            send(("as", i), hg.at[rows], hg.at[rows], sibling, "busy")

        for way, sign in signs:
            meet(mid - sign * reach)
            relay(way, sign, 0)
        for s in [mid] + first_slots:
            meet(s)
        send(("wi",), w_in_hbm, w_in2, x_lo_peer, "busy")
        send(("wo",), w_out_hbm, w_out2, x_lo_peer, "busy")
        for way, sign in signs:
            slot = mid - sign * reach
            arrived(("ax", slot), hg.at[tok(slot, rx=1)])
            relay(way, sign, 1)
        for s in [mid] + first_slots:
            arrived(("ax", s), hg.at[tok(s, rx=1)])
        down(0)
        for i in (1, 2):
            for s in range(spans[i][0], spans[i][0] + spans[i][1]):
                for rx in (0, 1):
                    if s == 0:
                        for way in (0, 1):
                            arrived(("az", 0, rx, way), hg.at[tok(0, rx), pl.ds(2 * f * way, 2 * f)])
                    else:
                        arrived(("az", s, rx), hg.at[tok(s, rx)])
            down(i)

    @pl.when(idle)
    def _():
        for i in range(3):
            rows = tok(spans[i][0], n=2 * spans[i][1])
            arrived(("as", i), hg.at[rows])

    def products():
        part[:, :f] = (jnp.dot(hg[:, :f], w_in[...], preferred_element_type=F32)
                       + jnp.dot(hg[:, 2 * f:3 * f], w_in2[...], preferred_element_type=F32)).astype(BF16)
        turned = (((1,), (1,)), ((), ()))
        part[:, f:] = (
            lax.dot_general(hg[:, f:2 * f], w_out[...], turned, preferred_element_type=F32)
            + lax.dot_general(hg[:, 3 * f:], w_out2[...], turned, preferred_element_type=F32)).astype(BF16)

    share = 2 * nz * blk // ny

    def owned(d, j=None):
        start = lax.rem(y + (d + ny), ny) * share
        if j is None:
            return pl.ds(pl.multiple_of(start, share), share)
        return pl.ds(pl.multiple_of(start + j * (share // 2), share // 2), share // 2)

    def stage(way, i, j=None):
        start = (way * hop + i - 1) * share
        return pl.ds(start, share) if j is None else pl.ds(start + j * (share // 2), share // 2)

    def c_first():
        for i in range(hop, 0, -1):
            for way, sign in signs:
                j = way if i == hop else None
                send(("c1", way, i), part.at[owned(sign * (hop + i), j)], c1_in.at[stage(way, i, j)], at_y(sign * i))
        for i in range(hop - 1, 0, -1):
            for way, sign in signs:
                send(("c2", way, i), part.at[owned(sign * i)], c2_in.at[stage(way, i)], at_y(sign * i))

    def c_relay():
        for way, sign in signs:
            out = pl.ds(way * share, share)
            last = stage(way, hop, way)
            total = part[owned(sign * hop), :].astype(F32)
            for i in range(1, hop):
                arrived(("c1", way, i), c1_in.at[stage(way, i)])
                total = total + c1_in[stage(way, i), :].astype(F32)
            arrived(("c1", way, hop), c1_in.at[last])
            c2_out[out, :] = total.astype(BF16)
            lo = way * (share // 2)
            c2_out[pl.ds(way * share + lo, share // 2), :] = (
                total[lo:lo + share // 2] + c1_in[last, :].astype(F32)).astype(BF16)
            send(("c2", way, hop), c2_out.at[out], c2_in.at[stage(way, hop)], at_y(sign * hop))

    def act():
        mine = owned(0)
        total = part[mine, :].astype(F32)
        for i in range(1, hop + 1):
            for way in (0, 1):
                arrived(("c2", way, i), c2_in.at[stage(way, i)])
                total = total + c2_in[stage(way, i), :].astype(F32)
        pre = total[:, :f] + b_in[...].reshape(1, f)
        cdf = 0.5 * (1.0 + lax.erf(pre * (1.0 / math.sqrt(2.0))))
        pdf = jnp.exp(-0.5 * pre * pre) * (1.0 / math.sqrt(2.0 * math.pi))
        ae[mine, :f] = (pre * cdf).astype(BF16)
        ae[mine, f:] = (total[:, f:] * (cdf + pre * pdf)).astype(BF16)
        for i in range(hop, 0, -1):
            for way, sign in signs:
                send(("e1", way, i), ae.at[mine], ae.at[mine], at_y(sign * i))

    def e_relay():
        for way, sign in signs:
            arrived(("e1", way, hop), ae.at[owned(-sign * hop)])
            for d in range(hop, 0, -1):
                rows = owned(-sign * hop, way if d == hop else None)
                send(("e2", way, d), ae.at[rows], ae.at[rows], at_y(sign * d))

    def input_grad(d):
        rows = owned(d)
        both = jnp.dot(ae[rows, f:], turned_in[...], preferred_element_type=F32)
        own, other = both[:, :f], both[:, f:]

        @pl.when(busy)
        def _():
            gn[rows, :] = own
            gn_give[rows, :] = other.astype(BF16)

        @pl.when(idle)
        def _():
            gn[rows, :] = other
            gn_give[rows, :] = own.astype(BF16)

        send(("gs", d % ny), gn_give.at[rows], gn_got.at[rows], sibling)

    def g_first(d):
        rows = owned(d)
        arrived(("gs", d % ny), gn_got.at[rows])
        gn[rows, :] = gn[rows, :] + gn_got[rows, :].astype(F32)
        gs[rows, :] = gn[rows, :].astype(BF16)

    def gather_and_grad():
        input_grad(0)
        e_relay()
        for way, sign in signs:
            input_grad(-sign * hop)
        g_first(0)
        for i in range(1, hop):
            for way, sign in signs:
                arrived(("e1", way, i), ae.at[owned(-sign * i)])
                input_grad(-sign * i)
        for way, sign in signs:
            g_first(-sign * hop)
        for d in range(1, hop):
            for way, sign in signs:
                arrived(("e2", way, d), ae.at[owned(-sign * (hop + d))])
                input_grad(-sign * (hop + d))
        for i in range(1, hop):
            for way, sign in signs:
                g_first(-sign * i)
        for way, sign in signs:
            arrived(("e2", way, hop), ae.at[owned(half, way)])
        input_grad(half)
        for d in range(1, hop):
            for way, sign in signs:
                g_first(-sign * (hop + d))
        g_first(half)

    def g_rows(way, i, j=None):
        start = (way * reach + i - 1) * 2 * blk
        return pl.ds(start, 2 * blk) if j is None else pl.ds(start + j * blk, blk)

    def g_send():
        for i in range(reach, 0, -1):
            for way, sign in signs:
                slot = (mid + sign * (reach + i)) % nz
                src, dst = (tok(slot, n=2), g_rows(way, i)) if i < reach else (tok(slot, rx=way), g_rows(way, i, way))
                send(("g1", way, i), gs.at[src], g1_in.at[dst], at_z(sign * i))
        for i in range(reach - 1, 0, -1):
            for way, sign in signs:
                send(("g2", way, i), gs.at[tok(mid + sign * i, n=2)], g2_in.at[g_rows(way, i)], at_z(sign * i))

    def g_relay():
        for way, sign in signs:
            total = gn[tok(mid + sign * reach, n=2), :]
            for i in range(1, reach):
                arrived(("g1", way, i), g1_in.at[g_rows(way, i)])
                total = total + g1_in[g_rows(way, i), :].astype(F32)
            last = g_rows(way, reach, way)
            arrived(("g1", way, reach), g1_in.at[last])
            there, out = g_rows(way, reach), pl.ds(way * 2 * blk, 2 * blk)
            g2_out[out, :] = total.astype(BF16)
            half_rows = pl.ds((way * 2 + way) * blk, blk)
            g2_out[half_rows, :] = (total[way * blk:(way + 1) * blk] + g1_in[last, :].astype(F32)).astype(BF16)
            send(("g2", way, reach), g2_out.at[out], g2_in.at[there], at_z(sign * reach))

    def g_end():
        total = gn[tok(mid, n=2), :]
        for i in range(1, reach + 1):
            for way in (0, 1):
                arrived(("g2", way, i), g2_in.at[g_rows(way, i)])
                total = total + g2_in[g_rows(way, i), :].astype(F32)
        g_out[...] = total.astype(BF16)
        first, second = pl.ds(0, blk), pl.ds(blk, blk)

        @pl.when(busy)
        def _():
            gn[pl.ds(0, blk), :] = total[:blk]
            send(("gx",), g_out.at[second], gx_in, x_hi_peer, "busy")

        @pl.when(idle)
        def _():
            send(("gx",), g_out.at[second], gx_in, cross_both, "idle")
            send(("gl",), g_out.at[first], gl_in, cross_lo, "idle")

    def g_result():
        arrived(("gx",), gx_in)

        @pl.when(busy)
        def _():
            o_normed[...] = (gn[pl.ds(0, blk), :] + gx_in[...].astype(F32)).astype(BF16)

        @pl.when(idle)
        def _():
            arrived(("gl",), gl_in)
            o_normed[...] = (gl_in[...].astype(F32) + gx_in[...].astype(F32)).astype(BF16)

    down_rows = (((0,), (0,)), ((), ()))

    def other_weight_grads():
        a, e = ae[:, :f], ae[:, f:]
        vo_out[...] = lax.dot_general(a, hg[:, 3 * f:], down_rows, preferred_element_type=F32).astype(BF16)
        send(("vo",), vo_out, vo_in, x_lo_peer)
        vi_out[...] = lax.dot_general(hg[:, 2 * f:3 * f], e, down_rows, preferred_element_type=F32).astype(BF16)
        send(("vi",), vi_out, vi_in, x_lo_peer)
        vb_out[...] = jnp.broadcast_to(jnp.sum(e.astype(F32), axis=0, keepdims=True), (8, f))
        send(("vb",), vb_out, vb_in, x_lo_peer)

    def weight_grads():
        a, e = ae[:, :f], ae[:, f:]
        o_w_out[...] = lax.dot_general(a, hg[:, f:2 * f], down_rows, preferred_element_type=F32)
        o_w_in[...] = lax.dot_general(hg[:, :f], e, down_rows, preferred_element_type=F32)

    def weight_grads_end():
        arrived(("vo",), vo_in)
        o_w_out[...] += vo_in[...].astype(F32)
        arrived(("vi",), vi_in)
        o_w_in[...] += vi_in[...].astype(F32)
        arrived(("vb",), vb_in)
        o_b_in[...] = (vb_out[:1, :] + vb_in[:1, :]).reshape(f)

    for load in loads[4:]:
        load.wait()
    arrived(("wi",), w_in2)
    arrived(("wo",), w_out2)
    products()
    c_first()
    turned_in[:, :f] = w_in[...].T
    turned_in[:, f:] = w_in2[...].T
    c_relay()
    act()
    gather_and_grad()
    g_send()
    other_weight_grads()
    g_relay()
    weight_grads()
    g_end()
    weight_grads_end()
    g_result()

    @pl.when(idle)
    def _():
        for key, src in sent["idle"]:
            handle(key, src).wait_send()

    @pl.when(busy)
    def _():
        for key, src in sent["busy"]:
            handle(key, src).wait_send()

    for key, src in sent["all"]:
        handle(key, src).wait_send()


def on_device(ny, nz, normed, upstream, loss_weight, w_in, b_in, w_out):
    blk, f = normed.shape
    half, reach = ny // 2, nz // 4
    n = len(copy_keys(ny, nz))
    rows = 2 * nz * blk
    share = rows // ny
    vmem, hbm = pl.BlockSpec(memory_space=pltpu.VMEM), pl.BlockSpec(memory_space=pl.ANY)
    outs = pl.pallas_call(
        functools.partial(kernel, ny, nz, blk, f),
        out_shape=(
            jax.ShapeDtypeStruct((blk, f), BF16),
            jax.ShapeDtypeStruct(w_in.shape, F32),
            jax.ShapeDtypeStruct((f,), F32),
            jax.ShapeDtypeStruct(w_out.shape, F32),
        ),
        in_specs=[hbm] * 6,
        out_specs=(vmem,) * 4,
        scratch_shapes=[
            pltpu.VMEM((blk, f), BF16),
            pltpu.VMEM((blk, f), BF16),
            pltpu.VMEM((1, blk), F32),
            pltpu.VMEM((f,), F32),
            pltpu.VMEM((f, f), BF16),
            pltpu.VMEM((f, f), BF16),
            pltpu.VMEM((f, f), BF16),
            pltpu.VMEM((f, f), BF16),
            pltpu.VMEM((f, 2 * f), BF16),
            pltpu.VMEM((rows, 4 * f), BF16),
            pltpu.VMEM((blk, 2 * f), BF16),
            pltpu.VMEM((rows, 2 * f), BF16),
            pltpu.VMEM((rows, 2 * f), BF16),
            pltpu.VMEM((half * share, 2 * f), BF16),
            pltpu.VMEM((2 * share, 2 * f), BF16),
            pltpu.VMEM((half * share, 2 * f), BF16),
            pltpu.VMEM((rows, f), F32),
            pltpu.VMEM((rows, f), BF16),
            pltpu.VMEM((rows, f), BF16),
            pltpu.VMEM((rows, f), BF16),
            pltpu.VMEM((2 * reach * 2 * blk, f), BF16),
            pltpu.VMEM((2 * 2 * blk, f), BF16),
            pltpu.VMEM((2 * reach * 2 * blk, f), BF16),
            pltpu.VMEM((2 * blk, f), BF16),
            pltpu.VMEM((blk, f), BF16),
            pltpu.VMEM((blk, f), BF16),
            pltpu.VMEM((f, f), BF16),
            pltpu.VMEM((f, f), BF16),
            pltpu.VMEM((f, f), BF16),
            pltpu.VMEM((f, f), BF16),
            pltpu.VMEM((8, f), F32),
            pltpu.VMEM((8, f), F32),
            pltpu.SemaphoreType.DMA((6,)),
            pltpu.SemaphoreType.DMA((n,)),
            pltpu.SemaphoreType.DMA((n,)),
        ],
        compiler_params=pltpu.CompilerParams(
            collective_id=0, has_side_effects=True, vmem_limit_bytes=32 * 2**20),
        name="mlp_backward",
    )(*[pltpu.with_memory_space_constraint(x, pltpu.HBM) for x in (
        normed, upstream, loss_weight.reshape(1, blk), w_in, b_in, w_out)])
    return outs[0], outs[1], outs[2], outs[3]


def solution(mesh):
    ny, nz = mesh.shape["row"] // 2, mesh.shape["col"] // 4
    return jax.shard_map(
        functools.partial(on_device, ny, nz),
        mesh=mesh,
        in_specs=(P("col", "row"), P("col", "row"), P("col"), P("row", "col"), P("col"), P("col", "row")),
        out_specs=(P("col", "row"), P("row", "col"), P("col"), P("col", "row")),
        check_vma=False,
    )
```

```python
import functools
import math

import jax
import jax.numpy as jnp
from jax import lax
from jax.experimental import pallas as pl
from jax.experimental.pallas import tpu as pltpu
from jax.sharding import PartitionSpec as P

BF16 = jnp.bfloat16
F32 = jnp.float32
MESH = pl.DeviceIdType.MESH


def copy_keys(ny, nz):
    half, reach = ny // 2, nz // 4
    ways = (0, 1)
    keys = [("wi",), ("wo",), ("al",)]
    keys += [("az", s, rx) for rx in ways for s in range(1, nz) if s != nz // 2]
    keys += [("az", 0, rx, way) for rx in ways for way in ways]
    keys += [("al", nz // 2 + s * d) for d in range(1, reach + 1) for s in (1, -1)]
    keys += [("ax", nz // 2 + d) for d in range(-reach, reach + 1)] + [("as", i) for i in range(3)]
    keys += [(kind, way, i) for kind in ("c1", "c2", "e1", "e2") for way in ways for i in range(1, half // 2 + 1)]
    keys += [("gs", d % ny) for d in range(ny)]
    keys += [(kind, way, i) for kind in ("g1", "g2") for way in ways for i in range(1, reach + 1)]
    keys += [("gx",), ("gl",), ("vi",), ("vo",), ("vb",)]
    return {key: i for i, key in enumerate(keys)}


def kernel(ny, nz, blk, f, normed_hbm, upstream_hbm, loss_weight_hbm, w_in_hbm, b_in_hbm, w_out_hbm,
           o_normed, o_w_in, o_b_in, o_w_out,
           normed, upstream, loss_weight, b_in, w_in, w_out, w_in2, w_out2, turned_in,
           hg, al_out, part, ae, c1_in, c2_out, c2_in, gn, gn_give, gn_got, gs, g1_in, g2_out, g2_in, g_out, gx_in, gl_in,
           vi_out, vi_in, vo_out, vo_in, vb_out, vb_in, load_sem, send_sem, recv_sem):
    ids = copy_keys(ny, nz)
    half, mid, reach = ny // 2, nz // 2, nz // 4
    hop = half // 2
    row, col = lax.axis_index("row"), lax.axis_index("col")
    y, xl = row // 2, row % 2
    z, low = col // 4, col % 4
    xh, core = low // 2, low % 2
    busy = core == xl
    idle = core != xl
    signs = ((0, 1), (1, -1))

    def at_z(o):
        return (row, lax.rem(z + (o + nz), nz) * 4 + low)

    def at_y(d):
        return (lax.rem(y + (d + ny), ny) * 2 + xl, col)

    x_lo_peer = (y * 2 + (1 - xl), col)
    x_hi_peer = (row, z * 4 + (1 - xh) * 2 + core)
    cross_lo = (y * 2 + (1 - xl), z * 4 + xh * 2 + (1 - core))
    cross_both = (y * 2 + (1 - xl), z * 4 + (1 - xh) * 2 + (1 - core))
    sibling = (row, z * 4 + xh * 2 + (1 - core))

    sent = {"all": [], "busy": [], "idle": []}

    def send(key, src, dst, device, who="all"):
        pltpu.make_async_remote_copy(
            src_ref=src, dst_ref=dst, send_sem=send_sem.at[ids[key]], recv_sem=recv_sem.at[ids[key]],
            device_id=device, device_id_type=MESH).start()
        sent[who].append((key, src))

    def handle(key, ref):
        return pltpu.make_async_remote_copy(
            src_ref=ref, dst_ref=ref, send_sem=send_sem.at[ids[key]], recv_sem=recv_sem.at[ids[key]],
            device_id=sibling, device_id_type=MESH)

    def flush(who, kept=()):
        for key, src in sent[who]:
            if key[0] not in kept:
                handle(key, src).wait_send()
        sent[who][:] = [(key, src) for key, src in sent[who] if key[0] in kept]

    def flush_both():
        @pl.when(busy)
        def _():
            flush("busy")

        @pl.when(idle)
        def _():
            flush("idle")

    def arrived(key, dst):
        handle(key, dst).wait_recv()

    barrier = pltpu.get_barrier_semaphore()
    toward = [s * d for d in range(reach, 0, -1) for s in (1, -1)]
    near = [at_y(sign * d) for d in range(1, hop + 1) for sign in (1, -1)]
    near += [x_lo_peer, x_hi_peer, sibling] + [at_z(o) for o in toward]
    along_z = [at_z(o) for o in toward]
    slanted = [(y * 2 + (1 - xl), at_z(o)[1]) for o in toward]
    crossed = [cross_lo, cross_both]
    for peer in slanted + near:
        pl.semaphore_signal(barrier, inc=1, device_id=peer, device_id_type=MESH)

    @pl.when(idle)
    def _():
        for peer in crossed:
            pl.semaphore_signal(barrier, inc=1, device_id=peer, device_id_type=MESH)

    pairs = ((normed_hbm, normed), (upstream_hbm, upstream), (loss_weight_hbm, loss_weight), (b_in_hbm, b_in),
             (w_in_hbm, w_in), (w_out_hbm, w_out))
    loads = [pltpu.make_async_copy(src, dst, load_sem.at[i]) for i, (src, dst) in enumerate(pairs)]
    for load in loads:
        load.start()
    for load in loads[:4]:
        load.wait()

    def tok(slot, rx=0, n=1):
        return pl.ds((slot * 2 + rx) * blk, n * blk)

    diagonal = lax.broadcasted_iota(jnp.int32, (blk, blk), 0) == lax.broadcasted_iota(jnp.int32, (blk, blk), 1)
    weight = jnp.sum(jnp.where(diagonal, jnp.broadcast_to(loss_weight[...], (blk, blk)), 0.0), axis=1, keepdims=True)
    weighted = (upstream[...].astype(F32) * weight).astype(BF16)

    slab0, slab1 = pl.ds(0, 2 * f), pl.ds(2 * f, 2 * f)
    first_slots = [mid + s * d for d in range(1, reach) for s in (1, -1)]
    spans = [(mid - reach, 2 * reach + 1), (mid + reach + 1, mid - reach - 1), (0, mid - reach)]

    @pl.when(idle)
    def _():
        al_out[:, :f] = normed[...]
        al_out[:, f:] = weighted
        pl.semaphore_wait(barrier, len(near) + len(slanted) + len(crossed))
        for o, peer in zip(toward, slanted):
            send(("al", mid - o), al_out, hg.at[tok(mid - o), slab1], peer, "idle")
        send(("al",), al_out, hg.at[tok(mid), slab1], x_lo_peer, "idle")
        send(("wi",), w_in_hbm, w_in2, x_lo_peer, "idle")
        send(("wo",), w_out_hbm, w_out2, x_lo_peer, "idle")

    @pl.when(busy)
    def _():
        hg[tok(mid), slab0] = jnp.concatenate([normed[...], weighted], axis=1)
        pl.semaphore_wait(barrier, len(near) + len(slanted))
        for o, peer in zip(toward, along_z):
            send(("az", mid - o, 0), hg.at[tok(mid), slab0], hg.at[tok(mid - o), slab0], peer, "busy")

    def relay(way, sign, rx):
        slot = mid - sign * reach
        for d in range(reach, 0, -1):
            there = (slot - sign * d) % nz
            src, dst = tok(slot, rx), tok(there, rx)
            if d < reach:
                send(("az", there, rx), hg.at[src], hg.at[dst], at_z(sign * d), "busy")
            else:
                lanes = pl.ds(2 * f * way, 2 * f)
                send(("az", 0, rx, way), hg.at[src, lanes], hg.at[dst, lanes], at_z(sign * d), "busy")

    @pl.when(busy)
    def _():
        def meet(slot):
            if slot != mid:
                arrived(("az", slot, 0), hg.at[tok(slot), slab0])
            arrived(("al",) if slot == mid else ("al", slot), hg.at[tok(slot), slab1])
            send(("ax", slot), hg.at[tok(slot)], hg.at[tok(slot, rx=1)], x_hi_peer, "busy")

        def down(i):
            rows = tok(spans[i][0], n=2 * spans[i][1])
            send(("as", i), hg.at[rows], hg.at[rows], sibling, "busy")

        for way, sign in signs:
            meet(mid - sign * reach)
            relay(way, sign, 0)
        for s in [mid] + first_slots:
            meet(s)
        send(("wi",), w_in_hbm, w_in2, x_lo_peer, "busy")
        send(("wo",), w_out_hbm, w_out2, x_lo_peer, "busy")
        for way, sign in signs:
            slot = mid - sign * reach
            arrived(("ax", slot), hg.at[tok(slot, rx=1)])
            relay(way, sign, 1)
        for s in [mid] + first_slots:
            arrived(("ax", s), hg.at[tok(s, rx=1)])
        down(0)
        for i in (1, 2):
            for s in range(spans[i][0], spans[i][0] + spans[i][1]):
                for rx in (0, 1):
                    if s == 0:
                        for way in (0, 1):
                            arrived(("az", 0, rx, way), hg.at[tok(0, rx), pl.ds(2 * f * way, 2 * f)])
                    else:
                        arrived(("az", s, rx), hg.at[tok(s, rx)])
            down(i)

    @pl.when(idle)
    def _():
        for i in range(3):
            rows = tok(spans[i][0], n=2 * spans[i][1])
            arrived(("as", i), hg.at[rows])

    def products(d):
        rows = owned(d)
        part[rows, :f] = (jnp.dot(hg[rows, :f], w_in[...], preferred_element_type=F32)
                          + jnp.dot(hg[rows, 2 * f:3 * f], w_in2[...], preferred_element_type=F32)).astype(BF16)
        turned = (((1,), (1,)), ((), ()))
        part[rows, f:] = (
            lax.dot_general(hg[rows, f:2 * f], w_out[...], turned, preferred_element_type=F32)
            + lax.dot_general(hg[rows, 3 * f:], w_out2[...], turned, preferred_element_type=F32)).astype(BF16)

    share = 2 * nz * blk // ny

    def owned(d, j=None):
        start = lax.rem(y + (d + ny), ny) * share
        if j is None:
            return pl.ds(pl.multiple_of(start, share), share)
        return pl.ds(pl.multiple_of(start + j * (share // 2), share // 2), share // 2)

    def stage(way, i, j=None):
        start = (way * hop + i - 1) * share
        return pl.ds(start, share) if j is None else pl.ds(start + j * (share // 2), share // 2)

    def c_first():
        for i in range(hop, 0, -1):
            for way, sign in signs:
                j = way if i == hop else None
                if i < hop or way == 0:
                    products(sign * (hop + i))
                send(("c1", way, i), part.at[owned(sign * (hop + i), j)], c1_in.at[stage(way, i, j)], at_y(sign * i))
        for i in range(hop - 1, 0, -1):
            for way, sign in signs:
                products(sign * i)
                send(("c2", way, i), part.at[owned(sign * i)], c2_in.at[stage(way, i)], at_y(sign * i))

    def c_relay():
        for way, sign in signs:
            out = pl.ds(way * share, share)
            last = stage(way, hop, way)
            total = part[owned(sign * hop), :].astype(F32)
            for i in range(1, hop):
                arrived(("c1", way, i), c1_in.at[stage(way, i)])
                total = total + c1_in[stage(way, i), :].astype(F32)
            arrived(("c1", way, hop), c1_in.at[last])
            c2_out[out, :] = total.astype(BF16)
            lo = way * (share // 2)
            c2_out[pl.ds(way * share + lo, share // 2), :] = (
                total[lo:lo + share // 2] + c1_in[last, :].astype(F32)).astype(BF16)
            send(("c2", way, hop), c2_out.at[out], c2_in.at[stage(way, hop)], at_y(sign * hop))

    def act():
        mine = owned(0)
        total = part[mine, :].astype(F32)
        for i in range(1, hop + 1):
            for way in (0, 1):
                arrived(("c2", way, i), c2_in.at[stage(way, i)])
                total = total + c2_in[stage(way, i), :].astype(F32)
        pre = total[:, :f] + b_in[...].reshape(1, f)
        cdf = 0.5 * (1.0 + lax.erf(pre * (1.0 / math.sqrt(2.0))))
        pdf = jnp.exp(-0.5 * pre * pre) * (1.0 / math.sqrt(2.0 * math.pi))
        ae[mine, :f] = (pre * cdf).astype(BF16)
        ae[mine, f:] = (total[:, f:] * (cdf + pre * pdf)).astype(BF16)
        for i in range(hop, 0, -1):
            for way, sign in signs:
                send(("e1", way, i), ae.at[mine], ae.at[mine], at_y(sign * i))

    def e_relay():
        for way, sign in signs:
            arrived(("e1", way, hop), ae.at[owned(-sign * hop)])
            for d in range(hop, 0, -1):
                rows = owned(-sign * hop, way if d == hop else None)
                send(("e2", way, d), ae.at[rows], ae.at[rows], at_y(sign * d))

    def input_grad(d):
        rows = owned(d)
        both = jnp.dot(ae[rows, f:], turned_in[...], preferred_element_type=F32)
        own, other = both[:, :f], both[:, f:]

        @pl.when(busy)
        def _():
            gn[rows, :] = own
            gn_give[rows, :] = other.astype(BF16)

        @pl.when(idle)
        def _():
            gn[rows, :] = other
            gn_give[rows, :] = own.astype(BF16)

        send(("gs", d % ny), gn_give.at[rows], gn_got.at[rows], sibling)

    def g_first(d):
        rows = owned(d)
        arrived(("gs", d % ny), gn_got.at[rows])
        gn[rows, :] = gn[rows, :] + gn_got[rows, :].astype(F32)
        gs[rows, :] = gn[rows, :].astype(BF16)

    def gather_and_grad():
        input_grad(0)
        e_relay()
        for way, sign in signs:
            input_grad(-sign * hop)
        g_first(0)
        for i in range(1, hop):
            for way, sign in signs:
                arrived(("e1", way, i), ae.at[owned(-sign * i)])
                input_grad(-sign * i)
        for way, sign in signs:
            g_first(-sign * hop)
        for d in range(1, hop):
            for way, sign in signs:
                arrived(("e2", way, d), ae.at[owned(-sign * (hop + d))])
                input_grad(-sign * (hop + d))
        for i in range(1, hop):
            for way, sign in signs:
                g_first(-sign * i)
        for way, sign in signs:
            arrived(("e2", way, hop), ae.at[owned(half, way)])
        input_grad(half)
        for d in range(1, hop):
            for way, sign in signs:
                g_first(-sign * (hop + d))
        g_first(half)

    def g_rows(way, i, j=None):
        start = (way * reach + i - 1) * 2 * blk
        return pl.ds(start, 2 * blk) if j is None else pl.ds(start + j * blk, blk)

    def g_send():
        for i in range(reach, 0, -1):
            for way, sign in signs:
                slot = (mid + sign * (reach + i)) % nz
                src, dst = (tok(slot, n=2), g_rows(way, i)) if i < reach else (tok(slot, rx=way), g_rows(way, i, way))
                send(("g1", way, i), gs.at[src], g1_in.at[dst], at_z(sign * i))
        for i in range(reach - 1, 0, -1):
            for way, sign in signs:
                send(("g2", way, i), gs.at[tok(mid + sign * i, n=2)], g2_in.at[g_rows(way, i)], at_z(sign * i))

    def g_relay():
        for way, sign in signs:
            total = gn[tok(mid + sign * reach, n=2), :]
            for i in range(1, reach):
                arrived(("g1", way, i), g1_in.at[g_rows(way, i)])
                total = total + g1_in[g_rows(way, i), :].astype(F32)
            last = g_rows(way, reach, way)
            arrived(("g1", way, reach), g1_in.at[last])
            there, out = g_rows(way, reach), pl.ds(way * 2 * blk, 2 * blk)
            g2_out[out, :] = total.astype(BF16)
            half_rows = pl.ds((way * 2 + way) * blk, blk)
            g2_out[half_rows, :] = (total[way * blk:(way + 1) * blk] + g1_in[last, :].astype(F32)).astype(BF16)
            send(("g2", way, reach), g2_out.at[out], g2_in.at[there], at_z(sign * reach))

    def g_end():
        total = gn[tok(mid, n=2), :]
        for i in range(1, reach + 1):
            for way in (0, 1):
                arrived(("g2", way, i), g2_in.at[g_rows(way, i)])
                total = total + g2_in[g_rows(way, i), :].astype(F32)
        g_out[...] = total.astype(BF16)
        first, second = pl.ds(0, blk), pl.ds(blk, blk)

        @pl.when(busy)
        def _():
            gn[pl.ds(0, blk), :] = total[:blk]
            send(("gx",), g_out.at[second], gx_in, x_hi_peer, "busy")

        @pl.when(idle)
        def _():
            send(("gx",), g_out.at[second], gx_in, cross_both, "idle")
            send(("gl",), g_out.at[first], gl_in, cross_lo, "idle")

    def g_result():
        arrived(("gx",), gx_in)

        @pl.when(busy)
        def _():
            o_normed[...] = (gn[pl.ds(0, blk), :] + gx_in[...].astype(F32)).astype(BF16)

        @pl.when(idle)
        def _():
            arrived(("gl",), gl_in)
            o_normed[...] = (gl_in[...].astype(F32) + gx_in[...].astype(F32)).astype(BF16)

    down_rows = (((0,), (0,)), ((), ()))

    def other_weight_grads():
        a, e = ae[:, :f], ae[:, f:]
        vo_out[...] = lax.dot_general(a, hg[:, 3 * f:], down_rows, preferred_element_type=F32).astype(BF16)
        send(("vo",), vo_out, vo_in, x_lo_peer)
        vi_out[...] = lax.dot_general(hg[:, 2 * f:3 * f], e, down_rows, preferred_element_type=F32).astype(BF16)
        send(("vi",), vi_out, vi_in, x_lo_peer)
        vb_out[...] = jnp.broadcast_to(jnp.sum(e.astype(F32), axis=0, keepdims=True), (8, f))
        send(("vb",), vb_out, vb_in, x_lo_peer)

    def weight_grads():
        a, e = ae[:, :f], ae[:, f:]
        o_w_out[...] = lax.dot_general(a, hg[:, f:2 * f], down_rows, preferred_element_type=F32)
        o_w_in[...] = lax.dot_general(hg[:, :f], e, down_rows, preferred_element_type=F32)

    def weight_grads_end():
        arrived(("vo",), vo_in)
        o_w_out[...] += vo_in[...].astype(F32)
        arrived(("vi",), vi_in)
        o_w_in[...] += vi_in[...].astype(F32)
        arrived(("vb",), vb_in)
        o_b_in[...] = (vb_out[:1, :] + vb_in[:1, :]).reshape(f)

    for load in loads[4:]:
        load.wait()
    arrived(("wi",), w_in2)
    arrived(("wo",), w_out2)
    c_first()
    for d in (hop, -hop, 0):
        products(d)
    turned_in[:, :f] = w_in[...].T
    turned_in[:, f:] = w_in2[...].T
    flush_both()
    c_relay()
    act()
    gather_and_grad()
    g_send()
    other_weight_grads()
    g_relay()
    weight_grads()
    flush("all", ("vo", "vi", "vb"))
    g_end()
    weight_grads_end()
    g_result()

    flush_both()
    flush("all")


def on_device(ny, nz, normed, upstream, loss_weight, w_in, b_in, w_out):
    blk, f = normed.shape
    half, reach = ny // 2, nz // 4
    n = len(copy_keys(ny, nz))
    rows = 2 * nz * blk
    share = rows // ny
    vmem, hbm = pl.BlockSpec(memory_space=pltpu.VMEM), pl.BlockSpec(memory_space=pl.ANY)
    outs = pl.pallas_call(
        functools.partial(kernel, ny, nz, blk, f),
        out_shape=(
            jax.ShapeDtypeStruct((blk, f), BF16),
            jax.ShapeDtypeStruct(w_in.shape, F32),
            jax.ShapeDtypeStruct((f,), F32),
            jax.ShapeDtypeStruct(w_out.shape, F32),
        ),
        in_specs=[hbm] * 6,
        out_specs=(vmem,) * 4,
        scratch_shapes=[
            pltpu.VMEM((blk, f), BF16),
            pltpu.VMEM((blk, f), BF16),
            pltpu.VMEM((1, blk), F32),
            pltpu.VMEM((f,), F32),
            pltpu.VMEM((f, f), BF16),
            pltpu.VMEM((f, f), BF16),
            pltpu.VMEM((f, f), BF16),
            pltpu.VMEM((f, f), BF16),
            pltpu.VMEM((f, 2 * f), BF16),
            pltpu.VMEM((rows, 4 * f), BF16),
            pltpu.VMEM((blk, 2 * f), BF16),
            pltpu.VMEM((rows, 2 * f), BF16),
            pltpu.VMEM((rows, 2 * f), BF16),
            pltpu.VMEM((half * share, 2 * f), BF16),
            pltpu.VMEM((2 * share, 2 * f), BF16),
            pltpu.VMEM((half * share, 2 * f), BF16),
            pltpu.VMEM((rows, f), F32),
            pltpu.VMEM((rows, f), BF16),
            pltpu.VMEM((rows, f), BF16),
            pltpu.VMEM((rows, f), BF16),
            pltpu.VMEM((2 * reach * 2 * blk, f), BF16),
            pltpu.VMEM((2 * 2 * blk, f), BF16),
            pltpu.VMEM((2 * reach * 2 * blk, f), BF16),
            pltpu.VMEM((2 * blk, f), BF16),
            pltpu.VMEM((blk, f), BF16),
            pltpu.VMEM((blk, f), BF16),
            pltpu.VMEM((f, f), BF16),
            pltpu.VMEM((f, f), BF16),
            pltpu.VMEM((f, f), BF16),
            pltpu.VMEM((f, f), BF16),
            pltpu.VMEM((8, f), F32),
            pltpu.VMEM((8, f), F32),
            pltpu.SemaphoreType.DMA((6,)),
            pltpu.SemaphoreType.DMA((n,)),
            pltpu.SemaphoreType.DMA((n,)),
        ],
        compiler_params=pltpu.CompilerParams(
            collective_id=0, has_side_effects=True, vmem_limit_bytes=32 * 2**20),
        name="mlp_backward",
    )(*[pltpu.with_memory_space_constraint(x, pltpu.HBM) for x in (
        normed, upstream, loss_weight.reshape(1, blk), w_in, b_in, w_out)])
    return outs[0], outs[1], outs[2], outs[3]


def solution(mesh):
    ny, nz = mesh.shape["row"] // 2, mesh.shape["col"] // 4
    return jax.shard_map(
        functools.partial(on_device, ny, nz),
        mesh=mesh,
        in_specs=(P("col", "row"), P("col", "row"), P("col"), P("row", "col"), P("col"), P("col", "row")),
        out_specs=(P("col", "row"), P("row", "col"), P("col"), P("col", "row")),
        check_vma=False,
    )
```

```python
import functools
import math

import jax
import jax.numpy as jnp
from jax import lax
from jax.experimental import pallas as pl
from jax.experimental.pallas import tpu as pltpu
from jax.sharding import PartitionSpec as P

BF16 = jnp.bfloat16
F32 = jnp.float32
MESH = pl.DeviceIdType.MESH


def copy_keys(ny, nz):
    half, reach = ny // 2, nz // 4
    ways = (0, 1)
    keys = [("wi",), ("wo",), ("al",)]
    keys += [("az", s, rx) for rx in ways for s in range(1, nz) if s != nz // 2]
    keys += [("az", 0, rx, way) for rx in ways for way in ways]
    keys += [("al", nz // 2 + s * d) for d in range(1, reach + 1) for s in (1, -1)]
    keys += [("ax", nz // 2 + d) for d in range(-reach, reach + 1)] + [("as", i) for i in range(3)]
    keys += [(kind, way, i) for kind in ("c1", "c2", "e1", "e2") for way in ways for i in range(1, half // 2 + 1)]
    keys += [("gs", d % ny) for d in range(ny)]
    keys += [(kind, way, i) for kind in ("g1", "g2") for way in ways for i in range(1, reach + 1)]
    keys += [("gx",), ("gl",), ("vi",), ("vo",), ("vb",)]
    return {key: i for i, key in enumerate(keys)}


def kernel(ny, nz, blk, f, normed_hbm, upstream_hbm, loss_weight_hbm, w_in_hbm, b_in_hbm, w_out_hbm,
           o_normed, o_w_in, o_b_in, o_w_out,
           normed, upstream, loss_weight, b_in, w_in, w_out, w_in2, w_out2, turned_in,
           hg, al_out, part, ae, c1_in, c2_out, c2_in, gn, gn_give, gn_got, gs, g1_in, g2_out, g2_in, g_out, gx_in, gl_in,
           vi_out, vi_in, vo_out, vo_in, vb_out, vb_in, load_sem, send_sem, recv_sem):
    ids = copy_keys(ny, nz)
    half, mid, reach = ny // 2, nz // 2, nz // 4
    hop = half // 2
    row, col = lax.axis_index("row"), lax.axis_index("col")
    y, xl = row // 2, row % 2
    z, low = col // 4, col % 4
    xh, core = low // 2, low % 2
    busy = core == xl
    idle = core != xl
    signs = ((0, 1), (1, -1))

    def at_z(o):
        return (row, lax.rem(z + (o + nz), nz) * 4 + low)

    def at_y(d):
        return (lax.rem(y + (d + ny), ny) * 2 + xl, col)

    x_lo_peer = (y * 2 + (1 - xl), col)
    x_hi_peer = (row, z * 4 + (1 - xh) * 2 + core)
    cross_lo = (y * 2 + (1 - xl), z * 4 + xh * 2 + (1 - core))
    cross_both = (y * 2 + (1 - xl), z * 4 + (1 - xh) * 2 + (1 - core))
    sibling = (row, z * 4 + xh * 2 + (1 - core))

    sent = {"all": [], "busy": [], "idle": []}

    def send(key, src, dst, device, who="all"):
        pltpu.make_async_remote_copy(
            src_ref=src, dst_ref=dst, send_sem=send_sem.at[ids[key]], recv_sem=recv_sem.at[ids[key]],
            device_id=device, device_id_type=MESH).start()
        sent[who].append((key, src))

    def handle(key, ref):
        return pltpu.make_async_remote_copy(
            src_ref=ref, dst_ref=ref, send_sem=send_sem.at[ids[key]], recv_sem=recv_sem.at[ids[key]],
            device_id=sibling, device_id_type=MESH)

    def flush(who, kept=()):
        for key, src in sent[who]:
            if key[0] not in kept:
                handle(key, src).wait_send()
        sent[who][:] = [(key, src) for key, src in sent[who] if key[0] in kept]

    def flush_both():
        @pl.when(busy)
        def _():
            flush("busy")

        @pl.when(idle)
        def _():
            flush("idle")

    def arrived(key, dst):
        handle(key, dst).wait_recv()

    barrier = pltpu.get_barrier_semaphore()
    toward = [s * d for d in range(reach, 0, -1) for s in (1, -1)]
    near = [at_y(sign * d) for d in range(1, hop + 1) for sign in (1, -1)]
    near += [x_lo_peer, x_hi_peer, sibling] + [at_z(o) for o in toward]
    along_z = [at_z(o) for o in toward]
    slanted = [(y * 2 + (1 - xl), at_z(o)[1]) for o in toward]
    crossed = [cross_lo, cross_both]
    for peer in slanted + near:
        pl.semaphore_signal(barrier, inc=1, device_id=peer, device_id_type=MESH)

    @pl.when(idle)
    def _():
        for peer in crossed:
            pl.semaphore_signal(barrier, inc=1, device_id=peer, device_id_type=MESH)

    pairs = ((normed_hbm, normed), (upstream_hbm, upstream), (loss_weight_hbm, loss_weight), (b_in_hbm, b_in),
             (w_in_hbm, w_in), (w_out_hbm, w_out))
    loads = [pltpu.make_async_copy(src, dst, load_sem.at[i]) for i, (src, dst) in enumerate(pairs)]
    for load in loads:
        load.start()
    for load in loads[:4]:
        load.wait()

    def tok(slot, rx=0, n=1):
        return pl.ds((slot * 2 + rx) * blk, n * blk)

    diagonal = lax.broadcasted_iota(jnp.int32, (blk, blk), 0) == lax.broadcasted_iota(jnp.int32, (blk, blk), 1)
    weight = jnp.sum(jnp.where(diagonal, jnp.broadcast_to(loss_weight[...], (blk, blk)), 0.0), axis=1, keepdims=True)
    weighted = (upstream[...].astype(F32) * weight).astype(BF16)

    slab0, slab1 = pl.ds(0, 2 * f), pl.ds(2 * f, 2 * f)
    first_slots = [mid + s * d for d in range(1, reach) for s in (1, -1)]
    spans = [(mid - reach, 2 * reach + 1), (mid + reach + 1, mid - reach - 1), (0, mid - reach)]

    @pl.when(idle)
    def _():
        al_out[:, :f] = normed[...]
        al_out[:, f:] = weighted
        pl.semaphore_wait(barrier, len(near) + len(slanted) + len(crossed))
        for o, peer in zip(toward, slanted):
            send(("al", mid - o), al_out, hg.at[tok(mid - o), slab1], peer, "idle")
        send(("al",), al_out, hg.at[tok(mid), slab1], x_lo_peer, "idle")
        send(("wi",), w_in_hbm, w_in2, x_lo_peer, "idle")
        send(("wo",), w_out_hbm, w_out2, x_lo_peer, "idle")

    @pl.when(busy)
    def _():
        hg[tok(mid), slab0] = jnp.concatenate([normed[...], weighted], axis=1)
        pl.semaphore_wait(barrier, len(near) + len(slanted))
        for o, peer in zip(toward, along_z):
            send(("az", mid - o, 0), hg.at[tok(mid), slab0], hg.at[tok(mid - o), slab0], peer, "busy")

    def relay(way, sign, rx):
        slot = mid - sign * reach
        for d in range(reach, 0, -1):
            there = (slot - sign * d) % nz
            src, dst = tok(slot, rx), tok(there, rx)
            if d < reach:
                send(("az", there, rx), hg.at[src], hg.at[dst], at_z(sign * d), "busy")
            else:
                lanes = pl.ds(2 * f * way, 2 * f)
                send(("az", 0, rx, way), hg.at[src, lanes], hg.at[dst, lanes], at_z(sign * d), "busy")

    @pl.when(busy)
    def _():
        def meet(slot):
            if slot != mid:
                arrived(("az", slot, 0), hg.at[tok(slot), slab0])
            arrived(("al",) if slot == mid else ("al", slot), hg.at[tok(slot), slab1])
            send(("ax", slot), hg.at[tok(slot)], hg.at[tok(slot, rx=1)], x_hi_peer, "busy")

        def down(i):
            rows = tok(spans[i][0], n=2 * spans[i][1])
            send(("as", i), hg.at[rows], hg.at[rows], sibling, "busy")

        for way, sign in signs:
            meet(mid - sign * reach)
            relay(way, sign, 0)
        for s in [mid] + first_slots:
            meet(s)
        send(("wi",), w_in_hbm, w_in2, x_lo_peer, "busy")
        send(("wo",), w_out_hbm, w_out2, x_lo_peer, "busy")
        for way, sign in signs:
            slot = mid - sign * reach
            arrived(("ax", slot), hg.at[tok(slot, rx=1)])
            relay(way, sign, 1)
        for s in [mid] + first_slots:
            arrived(("ax", s), hg.at[tok(s, rx=1)])
        down(0)
        for i in (1, 2):
            for s in range(spans[i][0], spans[i][0] + spans[i][1]):
                for rx in (0, 1):
                    if s == 0:
                        for way in (0, 1):
                            arrived(("az", 0, rx, way), hg.at[tok(0, rx), pl.ds(2 * f * way, 2 * f)])
                    else:
                        arrived(("az", s, rx), hg.at[tok(s, rx)])
            down(i)

    @pl.when(idle)
    def _():
        for i in range(3):
            rows = tok(spans[i][0], n=2 * spans[i][1])
            arrived(("as", i), hg.at[rows])

    def products(d):
        rows = owned(d)
        part[rows, :f] = (jnp.dot(hg[rows, :f], w_in[...], preferred_element_type=F32)
                          + jnp.dot(hg[rows, 2 * f:3 * f], w_in2[...], preferred_element_type=F32)).astype(BF16)
        turned = (((1,), (1,)), ((), ()))
        part[rows, f:] = (
            lax.dot_general(hg[rows, f:2 * f], w_out[...], turned, preferred_element_type=F32)
            + lax.dot_general(hg[rows, 3 * f:], w_out2[...], turned, preferred_element_type=F32)).astype(BF16)

    share = 2 * nz * blk // ny

    def owned(d, j=None):
        start = lax.rem(y + (d + ny), ny) * share
        if j is None:
            return pl.ds(pl.multiple_of(start, share), share)
        return pl.ds(pl.multiple_of(start + j * (share // 2), share // 2), share // 2)

    def stage(way, i, j=None):
        start = (way * hop + i - 1) * share
        return pl.ds(start, share) if j is None else pl.ds(start + j * (share // 2), share // 2)

    def c_first():
        for i in range(hop, 0, -1):
            for way, sign in signs:
                j = way if i == hop else None
                if i < hop or way == 0:
                    products(sign * (hop + i))
                send(("c1", way, i), part.at[owned(sign * (hop + i), j)], c1_in.at[stage(way, i, j)], at_y(sign * i))
        for i in range(hop - 1, 0, -1):
            for way, sign in signs:
                products(sign * i)
                send(("c2", way, i), part.at[owned(sign * i)], c2_in.at[stage(way, i)], at_y(sign * i))

    def c_relay():
        for way, sign in signs:
            out = pl.ds(way * share, share)
            last = stage(way, hop, way)
            total = part[owned(sign * hop), :].astype(F32)
            for i in range(1, hop):
                arrived(("c1", way, i), c1_in.at[stage(way, i)])
                total = total + c1_in[stage(way, i), :].astype(F32)
            arrived(("c1", way, hop), c1_in.at[last])
            c2_out[out, :] = total.astype(BF16)
            lo = way * (share // 2)
            c2_out[pl.ds(way * share + lo, share // 2), :] = (
                total[lo:lo + share // 2] + c1_in[last, :].astype(F32)).astype(BF16)
            send(("c2", way, hop), c2_out.at[out], c2_in.at[stage(way, hop)], at_y(sign * hop))

    def act():
        mine = owned(0)
        total = part[mine, :].astype(F32)
        for i in range(1, hop + 1):
            for way in (0, 1):
                arrived(("c2", way, i), c2_in.at[stage(way, i)])
                total = total + c2_in[stage(way, i), :].astype(F32)
        pre = total[:, :f] + b_in[...].reshape(1, f)
        cdf = 0.5 * (1.0 + lax.erf(pre * (1.0 / math.sqrt(2.0))))
        pdf = jnp.exp(-0.5 * pre * pre) * (1.0 / math.sqrt(2.0 * math.pi))
        ae[mine, :f] = (pre * cdf).astype(BF16)
        ae[mine, f:] = (total[:, f:] * (cdf + pre * pdf)).astype(BF16)
        for i in range(hop, 0, -1):
            for way, sign in signs:
                send(("e1", way, i), ae.at[mine], ae.at[mine], at_y(sign * i))

    def e_relay():
        for way, sign in signs:
            arrived(("e1", way, hop), ae.at[owned(-sign * hop)])
            for d in range(hop, 0, -1):
                rows = owned(-sign * hop, way if d == hop else None)
                send(("e2", way, d), ae.at[rows], ae.at[rows], at_y(sign * d))

    def input_grad(d):
        rows = owned(d)
        both = jnp.dot(ae[rows, f:], turned_in[...], preferred_element_type=F32)
        own, other = both[:, :f], both[:, f:]

        @pl.when(busy)
        def _():
            gn[rows, :] = own
            gn_give[rows, :] = other.astype(BF16)

        @pl.when(idle)
        def _():
            gn[rows, :] = other
            gn_give[rows, :] = own.astype(BF16)

        send(("gs", d % ny), gn_give.at[rows], gn_got.at[rows], sibling)

    def g_first(d):
        rows = owned(d)
        arrived(("gs", d % ny), gn_got.at[rows])
        gn[rows, :] = gn[rows, :] + gn_got[rows, :].astype(F32)
        gs[rows, :] = gn[rows, :].astype(BF16)

    def gather_and_grad():
        input_grad(0)
        e_relay()
        for way, sign in signs:
            input_grad(-sign * hop)
        g_first(0)
        for i in range(1, hop):
            for way, sign in signs:
                arrived(("e1", way, i), ae.at[owned(-sign * i)])
                input_grad(-sign * i)
        for way, sign in signs:
            g_first(-sign * hop)
        for d in range(1, hop):
            for way, sign in signs:
                arrived(("e2", way, d), ae.at[owned(-sign * (hop + d))])
                input_grad(-sign * (hop + d))
        for i in range(1, hop):
            for way, sign in signs:
                g_first(-sign * i)
        for way, sign in signs:
            arrived(("e2", way, hop), ae.at[owned(half, way)])
        input_grad(half)
        for d in range(1, hop):
            for way, sign in signs:
                g_first(-sign * (hop + d))
        g_first(half)

    def g_rows(way, i, j=None):
        start = (way * reach + i - 1) * 2 * blk
        return pl.ds(start, 2 * blk) if j is None else pl.ds(start + j * blk, blk)

    def g_send():
        for i in range(reach, 0, -1):
            for way, sign in signs:
                slot = (mid + sign * (reach + i)) % nz
                src, dst = (tok(slot, n=2), g_rows(way, i)) if i < reach else (tok(slot, rx=way), g_rows(way, i, way))
                send(("g1", way, i), gs.at[src], g1_in.at[dst], at_z(sign * i))
        for i in range(reach - 1, 0, -1):
            for way, sign in signs:
                send(("g2", way, i), gs.at[tok(mid + sign * i, n=2)], g2_in.at[g_rows(way, i)], at_z(sign * i))

    def g_relay():
        for way, sign in signs:
            total = gn[tok(mid + sign * reach, n=2), :]
            for i in range(1, reach):
                arrived(("g1", way, i), g1_in.at[g_rows(way, i)])
                total = total + g1_in[g_rows(way, i), :].astype(F32)
            last = g_rows(way, reach, way)
            arrived(("g1", way, reach), g1_in.at[last])
            there, out = g_rows(way, reach), pl.ds(way * 2 * blk, 2 * blk)
            g2_out[out, :] = total.astype(BF16)
            half_rows = pl.ds((way * 2 + way) * blk, blk)
            g2_out[half_rows, :] = (total[way * blk:(way + 1) * blk] + g1_in[last, :].astype(F32)).astype(BF16)
            send(("g2", way, reach), g2_out.at[out], g2_in.at[there], at_z(sign * reach))

    def g_end():
        total = gn[tok(mid, n=2), :]
        for i in range(1, reach + 1):
            for way in (0, 1):
                arrived(("g2", way, i), g2_in.at[g_rows(way, i)])
                total = total + g2_in[g_rows(way, i), :].astype(F32)
        g_out[...] = total.astype(BF16)
        first, second = pl.ds(0, blk), pl.ds(blk, blk)

        @pl.when(busy)
        def _():
            gn[pl.ds(0, blk), :] = total[:blk]
            send(("gx",), g_out.at[second], gx_in, x_hi_peer, "busy")

        @pl.when(idle)
        def _():
            send(("gx",), g_out.at[second], gx_in, cross_both, "idle")
            send(("gl",), g_out.at[first], gl_in, cross_lo, "idle")

    def g_result():
        arrived(("gx",), gx_in)

        @pl.when(busy)
        def _():
            o_normed[...] = (gn[pl.ds(0, blk), :] + gx_in[...].astype(F32)).astype(BF16)

        @pl.when(idle)
        def _():
            arrived(("gl",), gl_in)
            o_normed[...] = (gl_in[...].astype(F32) + gx_in[...].astype(F32)).astype(BF16)

    down_rows = (((0,), (0,)), ((), ()))

    def other_weight_grads():
        a, e = ae[:, :f], ae[:, f:]
        vo_out[...] = lax.dot_general(a, hg[:, 3 * f:], down_rows, preferred_element_type=F32).astype(BF16)
        send(("vo",), vo_out, vo_in, x_lo_peer)
        vi_out[...] = lax.dot_general(hg[:, 2 * f:3 * f], e, down_rows, preferred_element_type=F32).astype(BF16)
        send(("vi",), vi_out, vi_in, x_lo_peer)
        vb_out[...] = jnp.broadcast_to(jnp.sum(e.astype(F32), axis=0, keepdims=True), (8, f))
        send(("vb",), vb_out, vb_in, x_lo_peer)

    def weight_grads():
        a, e = ae[:, :f], ae[:, f:]
        o_w_out[...] = lax.dot_general(a, hg[:, f:2 * f], down_rows, preferred_element_type=F32)
        o_w_in[...] = lax.dot_general(hg[:, :f], e, down_rows, preferred_element_type=F32)

    def weight_grads_end():
        arrived(("vo",), vo_in)
        o_w_out[...] += vo_in[...].astype(F32)
        arrived(("vi",), vi_in)
        o_w_in[...] += vi_in[...].astype(F32)
        arrived(("vb",), vb_in)
        o_b_in[...] = (vb_out[:1, :] + vb_in[:1, :]).reshape(f)

    for load in loads[4:]:
        load.wait()
    arrived(("wi",), w_in2)
    arrived(("wo",), w_out2)
    c_first()
    for d in (hop, -hop):
        products(d)
    c_relay()
    products(0)
    turned_in[:, :f] = w_in[...].T
    turned_in[:, f:] = w_in2[...].T
    flush_both()
    act()
    gather_and_grad()
    g_send()
    other_weight_grads()
    g_relay()
    weight_grads()
    flush("all", ("vo", "vi", "vb"))
    g_end()
    weight_grads_end()
    g_result()

    flush_both()
    flush("all")


def on_device(ny, nz, normed, upstream, loss_weight, w_in, b_in, w_out):
    blk, f = normed.shape
    half, reach = ny // 2, nz // 4
    n = len(copy_keys(ny, nz))
    rows = 2 * nz * blk
    share = rows // ny
    vmem, hbm = pl.BlockSpec(memory_space=pltpu.VMEM), pl.BlockSpec(memory_space=pl.ANY)
    outs = pl.pallas_call(
        functools.partial(kernel, ny, nz, blk, f),
        out_shape=(
            jax.ShapeDtypeStruct((blk, f), BF16),
            jax.ShapeDtypeStruct(w_in.shape, F32),
            jax.ShapeDtypeStruct((f,), F32),
            jax.ShapeDtypeStruct(w_out.shape, F32),
        ),
        in_specs=[hbm] * 6,
        out_specs=(vmem,) * 4,
        scratch_shapes=[
            pltpu.VMEM((blk, f), BF16),
            pltpu.VMEM((blk, f), BF16),
            pltpu.VMEM((1, blk), F32),
            pltpu.VMEM((f,), F32),
            pltpu.VMEM((f, f), BF16),
            pltpu.VMEM((f, f), BF16),
            pltpu.VMEM((f, f), BF16),
            pltpu.VMEM((f, f), BF16),
            pltpu.VMEM((f, 2 * f), BF16),
            pltpu.VMEM((rows, 4 * f), BF16),
            pltpu.VMEM((blk, 2 * f), BF16),
            pltpu.VMEM((rows, 2 * f), BF16),
            pltpu.VMEM((rows, 2 * f), BF16),
            pltpu.VMEM((half * share, 2 * f), BF16),
            pltpu.VMEM((2 * share, 2 * f), BF16),
            pltpu.VMEM((half * share, 2 * f), BF16),
            pltpu.VMEM((rows, f), F32),
            pltpu.VMEM((rows, f), BF16),
            pltpu.VMEM((rows, f), BF16),
            pltpu.VMEM((rows, f), BF16),
            pltpu.VMEM((2 * reach * 2 * blk, f), BF16),
            pltpu.VMEM((2 * 2 * blk, f), BF16),
            pltpu.VMEM((2 * reach * 2 * blk, f), BF16),
            pltpu.VMEM((2 * blk, f), BF16),
            pltpu.VMEM((blk, f), BF16),
            pltpu.VMEM((blk, f), BF16),
            pltpu.VMEM((f, f), BF16),
            pltpu.VMEM((f, f), BF16),
            pltpu.VMEM((f, f), BF16),
            pltpu.VMEM((f, f), BF16),
            pltpu.VMEM((8, f), F32),
            pltpu.VMEM((8, f), F32),
            pltpu.SemaphoreType.DMA((6,)),
            pltpu.SemaphoreType.DMA((n,)),
            pltpu.SemaphoreType.DMA((n,)),
        ],
        compiler_params=pltpu.CompilerParams(
            collective_id=0, has_side_effects=True, vmem_limit_bytes=32 * 2**20),
        name="mlp_backward",
    )(*[pltpu.with_memory_space_constraint(x, pltpu.HBM) for x in (
        normed, upstream, loss_weight.reshape(1, blk), w_in, b_in, w_out)])
    return outs[0], outs[1], outs[2], outs[3]


def solution(mesh):
    ny, nz = mesh.shape["row"] // 2, mesh.shape["col"] // 4
    return jax.shard_map(
        functools.partial(on_device, ny, nz),
        mesh=mesh,
        in_specs=(P("col", "row"), P("col", "row"), P("col"), P("row", "col"), P("col"), P("col", "row")),
        out_specs=(P("col", "row"), P("row", "col"), P("col"), P("col", "row")),
        check_vma=False,
    )
```
